32 devices in a mesh: ctx: 4 (over z), ch: 8 (over y, x, core).
Axes of the slice: x: 2, y: 2, z: 4, core: 2. Of those that a mesh axis runs over, the one named last changes fastest.
Arguments:
- query_gate: bfloat16 [2048, 4096], P('ctx', 'ch'), may hold values from -6 to 6
- key_proj: bfloat16 [2048, 4096], P('ctx', 'ch'), may hold values from -6 to 6
- value_proj: bfloat16 [2048, 4096], P('ctx', 'ch'), may hold values from -6 to 6
- output_grad: bfloat16 [2048, 4096], P('ctx', 'ch'), may hold values from -6 to 6
- output_weight: bfloat16 [4096, 4096], P('ch'), may hold values from -0.09375 to 0.09375
- filter_taps: bfloat16 [2048, 4096], P('ctx', 'ch'), may hold values from -0.125 to 0.125
Outputs:
- grad_key: bfloat16 [2048, 4096], P('ctx', 'ch')
- grad_value: bfloat16 [2048, 4096], P('ctx', 'ch')
- grad_taps: float32 [2048, 4096], P('ctx', 'ch')
The draws below stay inside these ranges and needn't reach their ends.
All inputs are finite; a program needn't handle non-finite values.
Results may differ from the reference program's by a relative error of at most 0.012.
Values may be sent and summed in bfloat16 or wider, within the bound.
No kernel may reach another device: no remote copies, remote signals or barrier semaphores. Data moves between devices by JAX's collectives and lax.ppermute only.
A program may use at most 128 MiB of HBM per device.

```python
import math
import jax
import jax.numpy as jnp
from jax import lax

D = 4096
TOTAL = 2048


def steps_of(stream_key, shape, split, low, largest):
    loudness, own = 1.0, jax.random.fold_in(stream_key, 6)
    for dim, parts in split:
        steps = jnp.exp(jax.random.uniform(jax.random.fold_in(own, dim), (parts,), jnp.float32, low / len(split), largest / len(split)))
        loudness = loudness * jnp.repeat(steps, shape[dim] // parts).reshape([-1 if axis == dim else 1 for axis in range(len(shape))])
    return loudness


def normal_values(own_key, dims, spread, bound, shards=(), held_as=jnp.bfloat16):
    values = spread * jax.random.normal(own_key, dims, jnp.float32)
    if shards:
        values = values * steps_of(own_key, dims, shards, -0.22, 0.18)
    return jnp.clip(values, -bound, bound).astype(held_as)


def setup_inputs(seed: int = 0) -> dict:
    seeds = jax.random.split(jax.random.key(seed), 7)
    query_gate = normal_values(seeds[0], (TOTAL, D), 1.0, 6.0, ((0, 4), (1, 8)))
    key_proj = normal_values(seeds[1], (TOTAL, D), 1.0, 6.0, ((0, 4), (1, 8)))
    value_proj = normal_values(seeds[2], (TOTAL, D), 1.0, 6.0, ((0, 4), (1, 8)))
    output_grad = normal_values(seeds[3], (TOTAL, D), 1.0, 6.0, ((0, 4), (1, 8)))
    output_weight = normal_values(seeds[4], (D, D), D ** -0.5, 0.09375, ((0, 8),))
    filter_taps = normal_values(seeds[5], (TOTAL, D), TOTAL ** -0.5, 0.125, ((0, 4), (1, 8)))
    return {"query_gate": query_gate, "key_proj": key_proj, "value_proj": value_proj, "output_grad": output_grad, "output_weight": output_weight, "filter_taps": filter_taps}


def reference(query_gate, key_proj, value_proj, output_grad, output_weight, filter_taps):
    mixed_grad = jnp.dot(output_grad, output_weight.T, preferred_element_type=jnp.float32)
    conv_grad = (query_gate.astype(jnp.float32) * mixed_grad).astype(jnp.bfloat16)
    conv_grad = lax.optimization_barrier(conv_grad).astype(jnp.float32)
    product = (key_proj.astype(jnp.float32) * value_proj.astype(jnp.float32)).astype(jnp.bfloat16)
    inner = lax.optimization_barrier(product).astype(jnp.float32)
    period = 2 * TOTAL
    grad_spec = jnp.fft.rfft(conv_grad, n=period, axis=0)
    taps_spec = jnp.fft.rfft(filter_taps.astype(jnp.float32), n=period, axis=0)
    inner_spec = jnp.fft.rfft(inner, n=period, axis=0)
    input_grad = jnp.fft.irfft(jnp.conj(taps_spec) * grad_spec, n=period, axis=0)[:TOTAL]
    input_grad = input_grad.astype(jnp.float32)
    lagged = jnp.fft.irfft(jnp.conj(inner_spec) * grad_spec, n=period, axis=0)[:TOTAL]
    grad_taps = (lagged * (1.0 / math.sqrt(TOTAL))).astype(jnp.float32)
    grad_key = (value_proj.astype(jnp.float32) * input_grad).astype(jnp.bfloat16)
    grad_value = (key_proj.astype(jnp.float32) * input_grad).astype(jnp.bfloat16)
    return (grad_key, grad_value, grad_taps)
```

```python
import functools
import math

import jax
import jax.numpy as jnp
import ml_dtypes
import numpy as np
from jax import lax
from jax.experimental import pallas as pl
from jax.experimental.pallas import tpu as pltpu
from jax.sharding import PartitionSpec as P

BF16, F32 = jnp.bfloat16, jnp.float32
FOLDS = 16
LANES = 128


def spectral_tables(period):
    rows = period // FOLDS
    half = rows // 2
    place = np.arange(rows, dtype=np.int64)

    def angles(r):
        return 2.0 * np.pi * ((np.outer(FOLDS * place + r, place)) % period) / period

    forward_real = np.zeros((2, rows, rows))
    backward_real = np.zeros((2, rows, rows))
    for slot, r in ((0, 0), (1, FOLDS // 2)):
        a = angles(r)
        table = np.concatenate([np.cos(a[:half]), -np.sin(a[:half])], axis=0)
        if r == 0:
            table[half] = np.cos(a[half])
        forward_real[slot] = table
        inverse = table.T.copy()
        if r == 0:
            inverse[:, 0] *= 0.5
            inverse[:, half] *= 0.5
        backward_real[slot] = inverse
    forward, backward = [], []
    for r in range(1, FOLDS // 2):
        a = angles(r)
        forward.append(np.concatenate([np.cos(a), np.sin(a)], axis=0))
        backward.append(np.concatenate([np.cos(a).T, np.sin(a).T], axis=0))
    held = lambda t: np.asarray(t).astype(ml_dtypes.bfloat16)
    return held(forward_real), held(np.stack(forward)), held(backward_real), held(np.stack(backward))


def total(terms):
    terms = [t for t in terms if t is not None]
    while len(terms) > 1:
        terms = [a + b for a, b in zip(terms[::2], terms[1::2])] + ([terms[-1]] if len(terms) % 2 else [])
    return terms[0]


C1, S1, C2 = math.cos(math.pi / 8), math.sin(math.pi / 8), math.sqrt(0.5)


def fold_forward(x):
    u = [x[j] + x[j + 4] for j in range(4)]
    v = [x[j] - x[j + 4] for j in range(4)]
    u02, u13 = u[0] + u[2], u[1] + u[3]
    y = [None] * 9
    y[0] = (u02 + u13, None)
    y[8] = (u02 - u13, None)
    y[4] = (u[0] - u[2], u[3] - u[1])
    a, b = C2 * (v[1] - v[3]), C2 * (v[1] + v[3])
    y[2] = (v[0] + a, -(v[2] + b))
    y[6] = (v[0] - a, v[2] - b)
    for r, partner, sign, turns in ((1, 7, -1.0, ((C1, S1), (C2, C2), (S1, C1))), (3, 5, 1.0, ((S1, C1), (-C2, C2), (-C1, -S1)))):
        re, im = [x[0]], [x[4] if sign > 0 else -x[4]]
        for j, (c, s) in zip((1, 2, 3), turns):
            p, q = x[j], x[j + 4]
            if sign < 0:
                re.append(c * p - s * q)
                im.append(-(s * p + c * q))
            else:
                re.append(c * p + s * q)
                im.append(c * q - s * p)
        er, orr = re[0] + re[2], re[1] + re[3]
        ei, oi = im[0] + im[2], im[1] + im[3]
        y[r] = (er + orr, ei + oi)
        y[partner] = (er - orr, oi - ei)
    return y


def fold_backward(z):
    out = [None] * 8
    for parity in (0, 1):
        sign = 1.0 - 2.0 * parity
        a = {}
        for r in (1, 2, 3):
            zr, zi = z[r]
            pr, pi = z[8 - r]
            a[r] = (zr + pr, zi - pi) if parity == 0 else (zr - pr, zi + pi)
        base = z[0][0] + z[8][0] if parity == 0 else z[0][0] - z[8][0]
        z4r, z4i = z[4]
        a1r, a1i = a[1]
        a2r, a2i = a[2]
        a3r, a3i = a[3]
        if parity == 0:
            p0, p1 = base + z4r, base - z4r
            q0, q1 = p0 + a2r, p0 - a2r
            t0, t1 = p1 - a2i, p1 + a2i
            s = a1r + a3r
            out[0], d = q0 + s, None
            out[4] = q1 - a1i + a3i
            m, n = C2 * (a1r - a3r), C2 * (a1i + a3i)
            out[2] = t0 + m - n
            out[6] = t1 - m - n
        else:
            p0, p1 = base - z4i, base + z4i
            m, n = C2 * a2r, C2 * a2i
            e = {1: p0 + m - n, 3: p1 - m - n, 5: p0 - m + n, 7: p1 + m + n}
            c1r, s1r, c1i, s1i = C1 * a1r, S1 * a1r, C1 * a1i, S1 * a1i
            c3r, s3r, c3i, s3i = C1 * a3r, S1 * a3r, C1 * a3i, S1 * a3i
            out[1] = e[1] + (c1r - s1i) + (s3r - c3i)
            out[3] = e[3] + (s1r - c1i) + (-c3r + s3i)
            out[5] = e[5] + (-s1r - c1i) + (c3r + s3i)
            out[7] = e[7] + (-c1r - s1i) + (-s3r - c3i)
    return out


def pack_kernel(taps_ref, key_ref, value_ref, out_ref):
    for j in range(out_ref.shape[0]):
        cols = slice(j * LANES, (j + 1) * LANES)
        out_ref[j, :, :LANES] = taps_ref[:, cols]
        product = key_ref[:, cols].astype(F32) * value_ref[:, cols].astype(F32)
        out_ref[j, :, LANES:] = product.astype(BF16)


def spectrum_kernel(x_ref, real_ref, table_ref, out_ref, yr_ref, yi_ref):
    rows = real_ref.shape[1]
    step = 16

    def fold(i, carry):
        at = pl.multiple_of(i * step, step)
        x = [x_ref[pl.ds(j * rows + at, step), :].astype(F32) for j in range(8)]
        for r, (re, im) in enumerate(fold_forward(x)):
            yr_ref[r, pl.ds(at, step), :] = re.astype(BF16)
            if im is not None:
                yi_ref[r, pl.ds(at, step), :] = im.astype(BF16)
        return carry

    lax.fori_loop(0, rows // step, fold, 0)
    dot = functools.partial(jnp.dot, preferred_element_type=F32)
    out_ref[0, :rows] = dot(real_ref[0], yr_ref[0]).astype(out_ref.dtype)
    out_ref[0, rows:] = dot(real_ref[1], yr_ref[8]).astype(out_ref.dtype)
    for r in range(1, 8):
        a = dot(table_ref[r - 1], yr_ref[r])
        b = dot(table_ref[r - 1], yi_ref[r])
        out_ref[r, :rows] = (a[:rows] + b[rows:]).astype(out_ref.dtype)
        out_ref[r, rows:] = (b[:rows] - a[rows:]).astype(out_ref.dtype)


def correlate_kernel(ids_ref, g0, g1, g2, g3, spec_ref, fr_ref, f_ref, br_ref, b_ref, o0, o1, o2, o3, x_ref, y_ref, zr_ref, zi_ref, res_ref):
    rows = fr_ref.shape[1]
    half = rows // 2
    length = g0.shape[0]
    step = 16
    z = ids_ref[0]
    dot = functools.partial(jnp.dot, preferred_element_type=F32)
    for s, g in enumerate((g0, g1, g2, g3)):
        x_ref[pl.ds(pl.multiple_of((z ^ s) * length, length), length), :] = g[...]

    def fold(i, carry):
        at = pl.multiple_of(i * step, step)
        x = [x_ref[pl.ds(j * rows + at, step), :].astype(F32) for j in range(8)]
        y = fold_forward(x)
        y_ref[0, pl.ds(at, step), :LANES] = y[0][0].astype(BF16)
        y_ref[0, pl.ds(at, step), LANES:] = y[8][0].astype(BF16)
        for r in range(1, 8):
            y_ref[r, pl.ds(at, step), :LANES] = y[r][0].astype(BF16)
            y_ref[r, pl.ds(at, step), LANES:] = y[r][1].astype(BF16)
        return carry

    lax.fori_loop(0, rows // step, fold, 0)
    twice = lambda a: jnp.concatenate([a, a], axis=1)

    for r in range(1, 8):
        d = dot(f_ref[r - 1], y_ref[r])
        gr = twice(d[:rows, :LANES] + d[rows:, LANES:])
        gi = twice(d[:rows, LANES:] - d[rows:, :LANES])
        ar, ai = spec_ref[r, :rows].astype(F32), spec_ref[r, rows:].astype(F32)
        pr = (ar * gr + ai * gi).astype(BF16)
        pi = (ar * gi - ai * gr).astype(BF16)
        p = dot(b_ref[r - 1], pr)
        q = dot(b_ref[r - 1], pi)
        zr_ref[r] = p[:rows] - q[rows:]
        zi_ref[r] = q[:rows] + p[rows:]
    first = lax.broadcasted_iota(jnp.int32, (half, 2 * LANES), 0) == 0
    for slot, r in ((0, 0), (1, 8)):
        g = twice(dot(fr_ref[slot], y_ref[0, :, slot * LANES : (slot + 1) * LANES]))
        a = spec_ref[0, slot * rows : (slot + 1) * rows].astype(F32)
        gr, gi, ar, ai = g[:half], g[half:], a[:half], a[half:]
        pr = ar * gr + ai * gi
        pi = ar * gi - ai * gr
        if slot == 0:
            pr = jnp.where(first, ar * gr, pr)
            pi = jnp.where(first, ai * gi, pi)
        zr_ref[r] = dot(br_ref[slot], jnp.concatenate([pr, pi], axis=0).astype(BF16))
    scale = 1.0 / (FOLDS // 2 * rows)

    def unfold(i, carry):
        at = pl.multiple_of(i * step, step)
        for lane in (0, LANES):
            pick = lambda ref, r: ref[r, pl.ds(at, step), lane : lane + LANES]
            zs = [(pick(zr_ref, r), pick(zi_ref, r) if 0 < r < 8 else None) for r in range(9)]
            for j, out in enumerate(fold_backward(zs)):
                res_ref[pl.ds(j * rows + at, step), lane : lane + LANES] = (out * scale).astype(BF16)
        return carry

    lax.fori_loop(0, rows // step, unfold, 0)
    for s, o in enumerate((o0, o1, o2, o3)):
        o[...] = res_ref[pl.ds(pl.multiple_of((z ^ s) * length, length), length), :]


def finish_kernel(factor, ids_ref, r0, r1, r2, r3, key_ref, value_ref, gk_ref, gv_ref, gt_ref):
    z = ids_ref[0]
    for s, r in enumerate((r0, r1, r2, r3)):
        cols = pl.ds(pl.multiple_of((z ^ s) * LANES, LANES), LANES)
        grad = r[:, :LANES].astype(F32)
        gk_ref[:, cols] = (value_ref[:, cols].astype(F32) * grad).astype(BF16)
        gv_ref[:, cols] = (key_ref[:, cols].astype(F32) * grad).astype(BF16)
        gt_ref[:, cols] = r[:, LANES:].astype(F32) * factor


def project_kernel(n_weights, pairs, has_total, has_gate, ids_ref, *refs):
    refs = list(refs)
    weights = [refs.pop(0) for _ in range(n_weights)]
    blocks = [refs.pop(0) for _ in range(1 + max(p[0] for p in pairs))]
    before = refs.pop(0) if has_total else None
    gate = refs.pop(0) if has_gate else None
    sums = refs.pop() if has_gate else refs[0]
    rows = sums.shape[0]
    edges = sorted({p[2] for p in pairs}) + [rows]
    for lo, hi in zip(edges[:-1], edges[1:]):
        acc = before[lo:hi] if has_total else None
        for b, w, first in pairs:
            block = blocks[b]
            if not (first <= lo and hi <= first + block.shape[0]):
                continue
            part = lax.dot_general(block[lo - first : hi - first, :], weights[w][...], (((1,), (1,)), ((), ())), preferred_element_type=F32)
            acc = part if acc is None else acc + part
        sums[lo:hi] = acc
    if has_gate:
        z = ids_ref[0]
        for s, o in enumerate(refs):
            cols = pl.ds(pl.multiple_of((z ^ s) * LANES, LANES), LANES)
            o[...] = (gate[:, cols].astype(F32) * sums[:, cols]).astype(BF16)


VMEM = pl.BlockSpec(memory_space=pltpu.VMEM)
SMEM = pl.BlockSpec(memory_space=pltpu.SMEM)


def cost(flops, nbytes):
    return pl.CostEstimate(flops=flops, bytes_accessed=nbytes, transcendentals=0)


def limits(mib):
    return pltpu.CompilerParams(vmem_limit_bytes=mib * 2**20)


def project(ids, weight, offsets, blocks, pairs, before=None, gate=None, rows=None):
    channels = weight.shape[0]
    depth = blocks[0].shape[1]
    rows = rows or max(p[2] + blocks[p[0]].shape[0] for p in pairs)
    whole = lambda a: pl.BlockSpec(a.shape, lambda i, ids: (0, 0))
    ins = [weight] * len(offsets) + list(blocks)
    specs = [pl.BlockSpec((channels, depth), (lambda m: lambda i, ids: (0, ids[1] ^ m))(m)) for m in offsets]
    specs += [whole(b) for b in blocks]
    for extra in (before, gate):
        if extra is not None:
            ins.append(extra)
            specs.append(whole(extra))
    if gate is None:
        shapes = jax.ShapeDtypeStruct((rows, channels), F32)
        outs, scratch = whole(shapes), []
    else:
        shapes = [jax.ShapeDtypeStruct((rows, LANES), BF16)] * (channels // LANES)
        outs, scratch = [whole(s) for s in shapes], [pltpu.VMEM((rows, channels), F32)]
    kernel = functools.partial(project_kernel, len(offsets), tuple(pairs), before is not None, gate is not None)
    flops = 2 * sum(blocks[p[0]].shape[0] for p in pairs) * depth * channels
    return pl.pallas_call(
        kernel,
        grid_spec=pltpu.PrefetchScalarGridSpec(num_scalar_prefetch=1, grid=(1,), in_specs=specs, out_specs=outs, scratch_shapes=scratch),
        out_shape=shapes,
        compiler_params=limits(32),
        cost_estimate=cost(flops, sum(a.size * a.dtype.itemsize for a in ins[len(offsets):]) + 2 * len(offsets) * channels * depth),
    )(ids, *ins)


def pack(taps, key, value, parts):
    length = taps.shape[0]
    return pl.pallas_call(
        pack_kernel,
        out_shape=jax.ShapeDtypeStruct((parts, length, 2 * LANES), BF16),
        in_specs=[VMEM] * 3,
        out_specs=VMEM,
        compiler_params=limits(16),
        cost_estimate=cost(taps.size, 5 * 2 * taps.size),
    )(taps, key, value)


def block_spectrum(x, real, table):
    rows = real.shape[1]
    return pl.pallas_call(
        spectrum_kernel,
        out_shape=jax.ShapeDtypeStruct((8, 2 * rows, 2 * LANES), BF16),
        in_specs=[VMEM] * 3,
        out_specs=VMEM,
        scratch_shapes=[pltpu.VMEM((9, rows, 2 * LANES), BF16), pltpu.VMEM((8, rows, 2 * LANES), BF16)],
        compiler_params=limits(24),
        cost_estimate=cost(2 * 15 * 2 * rows * rows * 2 * LANES, 2 * (x.size + table.size + 16 * rows * 2 * LANES)),
    )(x, real, table)


def correlate(ids, grads, spec, tables):
    length = grads[0].shape[0]
    rows = tables[0].shape[1]
    return pl.pallas_call(
        correlate_kernel,
        out_shape=[jax.ShapeDtypeStruct((length, 2 * LANES), BF16)] * 4,
        in_specs=[SMEM] + [VMEM] * 9,
        out_specs=[VMEM] * 4,
        scratch_shapes=[
            pltpu.VMEM((8 * rows, LANES), BF16),
            pltpu.VMEM((8, rows, 2 * LANES), BF16),
            pltpu.VMEM((9, rows, 2 * LANES), F32),
            pltpu.VMEM((8, rows, 2 * LANES), F32),
            pltpu.VMEM((8 * rows, 2 * LANES), BF16),
        ],
        compiler_params=limits(32),
        cost_estimate=cost(2 * 8 * 6 * rows * rows * 2 * LANES, 2 * (4 * length * LANES * 3 + spec.size + 2 * tables[1].size)),
    )(ids, *grads, spec, *tables)


def finish(ids, parts, key, value, factor):
    shape = key.shape
    return pl.pallas_call(
        functools.partial(finish_kernel, factor),
        out_shape=[jax.ShapeDtypeStruct(shape, BF16), jax.ShapeDtypeStruct(shape, BF16), jax.ShapeDtypeStruct(shape, F32)],
        in_specs=[SMEM] + [VMEM] * 6,
        out_specs=[VMEM] * 3,
        compiler_params=limits(16),
        cost_estimate=cost(4 * key.size, 16 * key.size),
    )(ids, *parts, key, value)


PRECISION = lax.Precision.HIGH


def dft_tables(period):
    indices = jnp.arange(period, dtype=jnp.int32)
    product = indices[:, None] * indices[None, :] % period
    angles = product.astype(jnp.float32) * (2.0 * math.pi / period)
    return (jnp.cos(angles), jnp.sin(angles))


def spectrum(cosine_table, sine_table, framed_blocks):
    real_component = jnp.einsum(
        "br,irh->ibh", cosine_table, framed_blocks, precision=PRECISION
    )
    imaginary_component = -jnp.einsum(
        "br,irh->ibh", sine_table, framed_blocks, precision=PRECISION
    )
    return (real_component, imaginary_component)


def padded_spectrum(cosine_table, sine_table, blocks):
    framed_blocks = jnp.concatenate([blocks, jnp.zeros_like(blocks)], axis=1)
    return spectrum(cosine_table, sine_table, framed_blocks)


def inverse_rows(cosine_table, sine_table, real_component, imaginary_component, period):
    first_operand = jnp.einsum(
        "ir,qrb->qib", cosine_table, real_component, precision=PRECISION
    )
    second_operand = jnp.einsum(
        "ir,qrb->qib", sine_table, imaginary_component, precision=PRECISION
    )
    return (first_operand - second_operand) / period


def general_layer(query_gate, key_proj, value_proj, output_grad, output_weight, filter_taps):
    length = query_gate.shape[0]
    channels = query_gate.shape[1]
    period = 2 * length
    members = lax.axis_size("ctx")
    position = lax.axis_index("ctx")
    cosine_table, sine_table = dft_tables(period)
    mixed_grad = lax.dot_general(
        lax.all_gather(output_grad, "ch", axis=1, tiled=True),
        output_weight,
        (((1,), (1,)), ((), ())),
        preferred_element_type=jnp.float32,
    )
    conv_grad = (query_gate.astype(jnp.float32) * mixed_grad).astype(jnp.bfloat16)
    conv_grad = lax.optimization_barrier(conv_grad)
    product = (key_proj.astype(jnp.float32) * value_proj.astype(jnp.float32)).astype(jnp.bfloat16)
    product = lax.optimization_barrier(product)
    inner = product.astype(jnp.float32)
    inner_re, inner_im = padded_spectrum(cosine_table, sine_table, inner[None])
    inner_re = inner_re[0]
    inner_im = inner_im[0]
    whole_taps = lax.all_gather(filter_taps, "ctx", axis=0, tiled=True).astype(jnp.float32)
    leading = jnp.zeros((length, channels), jnp.float32)
    tap_blocks = jnp.concatenate([leading, whole_taps], axis=0).reshape(
        members + 1, length, channels
    )
    segments = jnp.concatenate([tap_blocks[:-1], tap_blocks[1:]], axis=1)
    segment_real, segment_imaginary = spectrum(cosine_table, sine_table, segments)
    lane_ids = jnp.arange(members, dtype=jnp.int32)
    blocks = (
        lax.all_gather(conv_grad, "ctx", axis=0, tiled=True)
        .astype(jnp.float32)
        .reshape(-1, length, channels)
    )
    anchor = jnp.arange(blocks.shape[0], dtype=jnp.int32)
    grad_re, grad_im = padded_spectrum(cosine_table, sine_table, blocks)
    offset = anchor - position
    select_entries = (offset[:, None] == lane_ids[None, :]).astype(jnp.float32)
    filter_tap_real = jnp.einsum(
        "so,owz->swz", select_entries, segment_real, precision=PRECISION
    )
    filter_tap_imaginary = jnp.einsum(
        "so,owz->swz", select_entries, segment_imaginary, precision=PRECISION
    )
    input_re = jnp.sum(filter_tap_real * grad_re + filter_tap_imaginary * grad_im, axis=0)
    input_im = jnp.sum(filter_tap_real * grad_im - filter_tap_imaginary * grad_re, axis=0)
    cross_re = inner_re * grad_re + inner_im * grad_im
    cross_im = inner_re * grad_im - inner_im * grad_re
    lagged = inverse_rows(cosine_table, sine_table, cross_re, cross_im, period)
    before = ((offset - 1)[:, None] == lane_ids[None, :]).astype(jnp.float32)
    upper = jnp.einsum(
        "pn,plc->nlc", select_entries, lagged[:, :length], precision=PRECISION
    )
    lower = jnp.einsum("pn,plc->nlc", before, lagged[:, length:], precision=PRECISION)
    input_grad = jnp.dot(
        cosine_table[length:], input_re, precision=PRECISION
    ) - jnp.dot(sine_table[length:], input_im, precision=PRECISION)
    input_grad = input_grad / period
    grad_key = (value_proj.astype(jnp.float32) * input_grad).astype(jnp.bfloat16)
    grad_value = (key_proj.astype(jnp.float32) * input_grad).astype(jnp.bfloat16)
    factor = 1.0 / math.sqrt(members * length)
    summed = lax.psum_scatter(
        (upper + lower).reshape(members * length, channels).astype(jnp.bfloat16),
        "ctx",
        scatter_dimension=0,
        tiled=True,
    ).astype(jnp.float32)
    grad_taps = summed * factor
    return (grad_key, grad_value, grad_taps)


def hop(x, axis, distance):
    n = lax.axis_size(axis)
    return lax.ppermute(x, axis, [(j, j ^ distance) for j in range(n)])


def exchanged_layer(query_gate, key_proj, value_proj, output_grad, output_weight, filter_taps):
    length, channels = query_gate.shape
    parts = lax.axis_size("ctx")
    tables = [jnp.asarray(t) for t in spectral_tables(2 * parts * length)]
    ids = jnp.stack([lax.axis_index("ctx"), lax.axis_index("ch")]).astype(jnp.int32)
    half = length // 2
    sent = pack(filter_taps, key_proj, value_proj, parts)
    from_x, from_y, from_core = hop(output_grad, "ch", 2), hop(output_grad, "ch", 4), hop(output_grad, "ch", 1)
    series = lax.all_to_all(sent, "ctx", 0, 0, tiled=True).reshape(parts * length, 2 * LANES)
    spec = block_spectrum(series, tables[0], tables[1])
    total = project(ids, output_weight, (0, 1), [output_grad, from_core], [(0, 0, 0), (1, 1, 0)])
    far_top, far_low = hop(from_y[:half], "ch", 2), hop(from_x[half:], "ch", 4)
    core_x, core_y = hop(from_x, "ch", 1), hop(from_y, "ch", 1)
    total = project(ids, output_weight, (2, 3, 4, 5), [from_x, core_x, from_y, core_y], [(j, j, 0) for j in range(4)], before=total)
    core_top, core_low = hop(far_top, "ch", 1), hop(far_low, "ch", 1)
    grads = project(ids, output_weight, (6, 7), [far_top, core_top, far_low, core_low], [(0, 0, 0), (1, 1, 0), (2, 0, half), (3, 1, half)], before=total, gate=query_gate)
    grads = [grads[0]] + [hop(grads[s], "ctx", s) for s in range(1, parts)]
    results = correlate(ids, grads, spec, tables)
    results = [results[0]] + [hop(results[s], "ctx", s) for s in range(1, parts)]
    return tuple(finish(ids, results, key_proj, value_proj, 1.0 / math.sqrt(parts * length)))


def per_device(*arrays):
    length, channels = arrays[0].shape
    if lax.axis_size("ctx") == 4 and lax.axis_size("ch") == 8 and channels == 4 * LANES and length % 32 == 0:
        return exchanged_layer(*arrays)
    return general_layer(*arrays)


def solution(mesh):
    return jax.shard_map(
        per_device,
        mesh=mesh,
        in_specs=(
            P("ctx", "ch"),
            P("ctx", "ch"),
            P("ctx", "ch"),
            P("ctx", "ch"),
            P("ch", None),
            P("ctx", "ch"),
        ),
        out_specs=(P("ctx", "ch"), P("ctx", "ch"), P("ctx", "ch")),
        check_vma=False,
    )
```

```python
import functools
import math

import jax
import jax.numpy as jnp
import ml_dtypes
import numpy as np
from jax import lax
from jax.experimental import pallas as pl
from jax.experimental.pallas import tpu as pltpu
from jax.sharding import PartitionSpec as P

BF16, F32 = jnp.bfloat16, jnp.float32
FOLDS = 16
LANES = 128


def spectral_tables(period):
    rows = period // FOLDS
    half = rows // 2
    place = np.arange(rows, dtype=np.int64)

    def angles(r):
        return 2.0 * np.pi * ((np.outer(FOLDS * place + r, place)) % period) / period

    forward_real = np.zeros((2, rows, rows))
    backward_real = np.zeros((2, rows, rows))
    for slot, r in ((0, 0), (1, FOLDS // 2)):
        a = angles(r)
        table = np.concatenate([np.cos(a[:half]), -np.sin(a[:half])], axis=0)
        if r == 0:
            table[half] = np.cos(a[half])
        forward_real[slot] = table
        inverse = table.T.copy()
        if r == 0:
            inverse[:, 0] *= 0.5
            inverse[:, half] *= 0.5
        backward_real[slot] = inverse
    forward, backward = [], []
    for r in range(1, FOLDS // 2):
        a = angles(r)
        forward.append(np.concatenate([np.cos(a), np.sin(a)], axis=0))
        backward.append(np.concatenate([np.cos(a).T, np.sin(a).T], axis=0))
    held = lambda t: np.asarray(t).astype(ml_dtypes.bfloat16)
    return held(forward_real), held(np.stack(forward)), held(backward_real), held(np.stack(backward))


def total(terms):
    terms = [t for t in terms if t is not None]
    while len(terms) > 1:
        terms = [a + b for a, b in zip(terms[::2], terms[1::2])] + ([terms[-1]] if len(terms) % 2 else [])
    return terms[0]


C1, S1, C2 = math.cos(math.pi / 8), math.sin(math.pi / 8), math.sqrt(0.5)


def fold_forward(x):
    u = [x[j] + x[j + 4] for j in range(4)]
    v = [x[j] - x[j + 4] for j in range(4)]
    u02, u13 = u[0] + u[2], u[1] + u[3]
    y = [None] * 9
    y[0] = (u02 + u13, None)
    y[8] = (u02 - u13, None)
    y[4] = (u[0] - u[2], u[3] - u[1])
    a, b = C2 * (v[1] - v[3]), C2 * (v[1] + v[3])
    y[2] = (v[0] + a, -(v[2] + b))
    y[6] = (v[0] - a, v[2] - b)
    for r, partner, sign, turns in ((1, 7, -1.0, ((C1, S1), (C2, C2), (S1, C1))), (3, 5, 1.0, ((S1, C1), (-C2, C2), (-C1, -S1)))):
        re, im = [x[0]], [x[4] if sign > 0 else -x[4]]
        for j, (c, s) in zip((1, 2, 3), turns):
            p, q = x[j], x[j + 4]
            if sign < 0:
                re.append(c * p - s * q)
                im.append(-(s * p + c * q))
            else:
                re.append(c * p + s * q)
                im.append(c * q - s * p)
        er, orr = re[0] + re[2], re[1] + re[3]
        ei, oi = im[0] + im[2], im[1] + im[3]
        y[r] = (er + orr, ei + oi)
        y[partner] = (er - orr, oi - ei)
    return y


def fold_backward(z):
    out = [None] * 8
    for parity in (0, 1):
        sign = 1.0 - 2.0 * parity
        a = {}
        for r in (1, 2, 3):
            zr, zi = z[r]
            pr, pi = z[8 - r]
            a[r] = (zr + pr, zi - pi) if parity == 0 else (zr - pr, zi + pi)
        base = z[0][0] + z[8][0] if parity == 0 else z[0][0] - z[8][0]
        z4r, z4i = z[4]
        a1r, a1i = a[1]
        a2r, a2i = a[2]
        a3r, a3i = a[3]
        if parity == 0:
            p0, p1 = base + z4r, base - z4r
            q0, q1 = p0 + a2r, p0 - a2r
            t0, t1 = p1 - a2i, p1 + a2i
            s = a1r + a3r
            out[0], d = q0 + s, None
            out[4] = q1 - a1i + a3i
            m, n = C2 * (a1r - a3r), C2 * (a1i + a3i)
            out[2] = t0 + m - n
            out[6] = t1 - m - n
        else:
            p0, p1 = base - z4i, base + z4i
            m, n = C2 * a2r, C2 * a2i
            e = {1: p0 + m - n, 3: p1 - m - n, 5: p0 - m + n, 7: p1 + m + n}
            c1r, s1r, c1i, s1i = C1 * a1r, S1 * a1r, C1 * a1i, S1 * a1i
            c3r, s3r, c3i, s3i = C1 * a3r, S1 * a3r, C1 * a3i, S1 * a3i
            out[1] = e[1] + (c1r - s1i) + (s3r - c3i)
            out[3] = e[3] + (s1r - c1i) + (-c3r + s3i)
            out[5] = e[5] + (-s1r - c1i) + (c3r + s3i)
            out[7] = e[7] + (-c1r - s1i) + (-s3r - c3i)
    return out


HALF = LANES // 2


def low_lanes(shape):
    return lax.broadcasted_iota(jnp.int32, shape, 1) < HALF


def swap_halves(a):
    return pltpu.roll(a, HALF, 1)


def join_low(a, b):
    return jnp.where(low_lanes(a.shape), a, swap_halves(b))


def join_high(a, b):
    return jnp.where(low_lanes(a.shape), swap_halves(a), b)


def pack_kernel(taps_hbm, key_hbm, value_hbm, out_hbm, taps_ref, key_ref, value_ref, out_ref, in_sems, out_sems):
    parts = out_ref.shape[0]
    reads = []
    for j in range(parts):
        cols = pl.ds(j * LANES, LANES)
        for i, (src, dst) in enumerate(((key_hbm, key_ref), (value_hbm, value_ref), (taps_hbm, taps_ref))):
            reads.append(pltpu.make_async_copy(src.at[:, cols], dst.at[j], in_sems.at[i, j]))
            reads[-1].start()
    writes = []
    for j in range(parts):
        for read in reads[3 * j : 3 * j + 3]:
            read.wait()
        inner = key_ref[j].astype(F32) * value_ref[j].astype(F32)
        taps = taps_ref[j].astype(F32)
        out_ref[j, :, :LANES] = join_low(taps, inner).astype(BF16)
        out_ref[j, :, LANES:] = join_high(taps, inner).astype(BF16)
        writes.append(pltpu.make_async_copy(out_ref.at[j], out_hbm.at[j], out_sems.at[j]))
        writes[-1].start()
    for write in writes:
        write.wait()


def fold_into(y_ref, x_ref, lane=0):
    rows, step = y_ref.shape[1], 16

    def fold(i, carry):
        at = pl.multiple_of(i * step, step)
        y = fold_forward([x_ref[pl.ds(j * rows + at, step), lane : lane + LANES].astype(F32) for j in range(8)])
        for r in range(8):
            left, right = y[r] if r else (y[0][0], y[8][0])
            y_ref[r, pl.ds(at, step), :LANES] = left.astype(BF16)
            y_ref[r, pl.ds(at, step), LANES:] = right.astype(BF16)
        return carry

    lax.fori_loop(0, rows // step, fold, 0, unroll=rows // step)


def dot(a, b):
    return jnp.dot(a, b, preferred_element_type=F32)


def spectrum_kernel(lane, x_ref, real_ref, table_ref, out_ref, y_ref):
    rows = real_ref.shape[1]
    fold_into(y_ref, x_ref, lane)
    out_ref[0, :rows] = dot(real_ref[0], y_ref[0, :, :LANES]).astype(out_ref.dtype)
    out_ref[0, rows:] = dot(real_ref[1], y_ref[0, :, LANES:]).astype(out_ref.dtype)
    for r in range(1, 8):
        d = dot(table_ref[r - 1], y_ref[r])
        out_ref[r, :rows] = (d[:rows, :LANES] + d[rows:, LANES:]).astype(out_ref.dtype)
        out_ref[r, rows:] = (d[:rows, LANES:] - d[rows:, :LANES]).astype(out_ref.dtype)


def correlate_kernel(ids_ref, g0, g1, g2, g3, spec_ref, fr_ref, f_ref, br_ref, b_ref, o0, o1, o2, o3, x_ref, y_ref, zr_ref, zi_ref, res_ref):
    rows = fr_ref.shape[1]
    half = rows // 2
    length = 2 * rows
    step = 16
    z = ids_ref[0]
    for s, g in enumerate((g0, g1, g2, g3)):
        start = pl.multiple_of((z ^ s) * length, length)
        both = g[...].astype(F32)
        x_ref[pl.ds(start, rows), :] = join_low(both, both).astype(BF16)
        x_ref[pl.ds(start + rows, rows), :] = join_high(both, both).astype(BF16)

    fold_into(y_ref, x_ref)
    beside = lambda a, b: jnp.concatenate([a, b], axis=1).astype(BF16)

    for r in range(1, 8):
        d = dot(f_ref[r - 1], y_ref[r])
        gr = d[:rows, :LANES] + d[rows:, LANES:]
        gi = d[:rows, LANES:] - d[rows:, :LANES]
        ar, ai = spec_ref[r, :rows].astype(F32), spec_ref[r, rows:].astype(F32)
        p = dot(b_ref[r - 1], beside(ar * gr + ai * gi, ar * gi - ai * gr))
        zr_ref[r] = p[:rows, :LANES] - p[rows:, LANES:]
        zi_ref[r] = p[:rows, LANES:] + p[rows:, :LANES]
    first = lax.broadcasted_iota(jnp.int32, (half, LANES), 0) == 0
    for slot, r in ((0, 0), (1, 8)):
        g = dot(fr_ref[slot], y_ref[0, :, slot * LANES : (slot + 1) * LANES])
        a = spec_ref[0, slot * rows : (slot + 1) * rows].astype(F32)
        gr, gi, ar, ai = g[:half], g[half:], a[:half], a[half:]
        pr = ar * gr + ai * gi
        pi = ar * gi - ai * gr
        if slot == 0:
            pr = jnp.where(first, ar * gr, pr)
            pi = jnp.where(first, ai * gi, pi)
        zr_ref[r] = dot(br_ref[slot], jnp.concatenate([pr, pi], axis=0).astype(BF16))
    scale = 1.0 / (FOLDS // 2 * rows)

    def unfold(i, carry):
        at = pl.multiple_of(i * step, step)
        zs = [(zr_ref[r, pl.ds(at, step), :], zi_ref[r, pl.ds(at, step), :] if 0 < r < 8 else None) for r in range(9)]
        for j, out in enumerate(fold_backward(zs)):
            res_ref[pl.ds(j * rows + at, step), :] = (out * scale).astype(BF16)
        return carry

    lax.fori_loop(0, rows // step, unfold, 0, unroll=rows // step)
    for s, o in enumerate((o0, o1, o2, o3)):
        o[...] = res_ref[pl.ds(pl.multiple_of((z ^ s) * length, length), length), :]


def finish_kernel(factor, ids_ref, *refs):
    lows, highs = refs[:4], refs[4:8]
    key_ref, value_ref, gk_ref, gv_ref, gt_ref = refs[8:]
    z = ids_ref[0]
    for s in range(4):
        low, high = lows[s][...].astype(F32), highs[s][...].astype(F32)
        cols = pl.ds(pl.multiple_of((z ^ s) * LANES, LANES), LANES)
        gt_ref[:, cols] = join_high(low, high) * factor
        grad = join_low(low, high)
        gk_ref[:, cols] = (value_ref[:, cols].astype(F32) * grad).astype(BF16)
        gv_ref[:, cols] = (key_ref[:, cols].astype(F32) * grad).astype(BF16)


def project_near_kernel(ids_ref, weight_ref, *refs):
    *blocks, sums, turned = refs
    depth = blocks[0].shape[1]

    def weight(distance):
        return weight_ref[:, pl.ds(pl.multiple_of((ids_ref[1] ^ distance) * depth, depth), depth)]

    acc = None
    for distance, block in enumerate(blocks):
        part = lax.dot_general(block[...], weight(distance), (((1,), (1,)), ((), ())), preferred_element_type=F32)
        acc = part if acc is None else acc + part
    sums[...] = acc
    for i in range(2):
        turned[i * depth : (i + 1) * depth] = weight(len(blocks) + i).T


def project_far_kernel(ids_ref, turned_ref, top0, top1, low0, low1, before, gate, *refs):
    outs, (block, sums) = refs[:-2], refs[-2:]
    half, depth = top0.shape
    for i, (top, low) in enumerate(((top0, low0), (top1, low1))):
        block[:half, i * depth : (i + 1) * depth] = top[...]
        block[half:, i * depth : (i + 1) * depth] = low[...]
    sums[...] = before[...] + dot(block[...], turned_ref[...])
    z = ids_ref[0]
    for s in range(4):
        cols = pl.ds(pl.multiple_of((z ^ s) * LANES, LANES), LANES)
        grad = gate[:, cols].astype(F32) * sums[:, cols]
        outs[s][...] = join_low(grad[:half], grad[half:]).astype(BF16)
        outs[4 + s][...] = join_high(grad[:half], grad[half:]).astype(BF16)


VMEM = pl.BlockSpec(memory_space=pltpu.VMEM)
SMEM = pl.BlockSpec(memory_space=pltpu.SMEM)
ANY = pl.BlockSpec(memory_space=pl.ANY)


def cost(flops, nbytes):
    return pl.CostEstimate(flops=flops, bytes_accessed=nbytes, transcendentals=0)


def limits(mib):
    return pltpu.CompilerParams(vmem_limit_bytes=mib * 2**20)


def project_near(ids, weight, blocks, hint):
    channels = weight.shape[0]
    rows, depth = blocks[0].shape
    return pl.pallas_call(
        project_near_kernel,
        in_specs=[SMEM] + [VMEM] * (1 + len(blocks)),
        out_specs=[VMEM] * 2,
        out_shape=[jax.ShapeDtypeStruct((rows, channels), F32), jax.ShapeDtypeStruct((2 * depth, channels), BF16)],
        compiler_params=limits(24),
        cost_estimate=cost(int(hint), 0),
    )(ids, weight, *blocks)


def project_far(ids, turned, blocks, before, gate):
    rows, channels = gate.shape
    return pl.pallas_call(
        project_far_kernel,
        in_specs=[SMEM] + [VMEM] * 7,
        out_specs=[VMEM] * 8,
        out_shape=[jax.ShapeDtypeStruct((rows // 2, LANES), BF16)] * 8,
        scratch_shapes=[pltpu.VMEM((rows, turned.shape[0]), BF16), pltpu.VMEM((rows, channels), F32)],
        compiler_params=limits(24),
        cost_estimate=cost(2 * rows * turned.size, 0),
    )(ids, turned, *blocks, before, gate)


def pack(taps, key, value, parts):
    length = taps.shape[0]
    shape = (parts, length, 2 * LANES)
    return pl.pallas_call(
        pack_kernel,
        out_shape=jax.ShapeDtypeStruct(shape, BF16),
        in_specs=[ANY] * 3,
        out_specs=ANY,
        scratch_shapes=[pltpu.VMEM((parts, length, LANES), BF16)] * 3
        + [pltpu.VMEM(shape, BF16), pltpu.SemaphoreType.DMA((3, parts)), pltpu.SemaphoreType.DMA((parts,))],
        compiler_params=limits(56),
        cost_estimate=cost(0, 10 * taps.size),
    )(taps, key, value)


def block_spectrum(x, lane, real, table):
    rows = real.shape[1]
    return pl.pallas_call(
        functools.partial(spectrum_kernel, lane),
        out_shape=jax.ShapeDtypeStruct((8, 2 * rows, LANES), BF16),
        in_specs=[VMEM] * 3,
        out_specs=VMEM,
        scratch_shapes=[pltpu.VMEM((8, rows, 2 * LANES), BF16)],
        compiler_params=limits(24),
        cost_estimate=cost(2 * 8 * 2 * rows * rows * 2 * LANES, 0),
    )(x, real, table)


def correlate(ids, grads, spec, tables):
    rows = tables[0].shape[1]
    length = 2 * rows
    return pl.pallas_call(
        correlate_kernel,
        out_shape=[jax.ShapeDtypeStruct((length, LANES), BF16)] * 4,
        in_specs=[SMEM] + [VMEM] * 9,
        out_specs=[VMEM] * 4,
        scratch_shapes=[
            pltpu.VMEM((8 * rows, LANES), BF16),
            pltpu.VMEM((8, rows, 2 * LANES), BF16),
            pltpu.VMEM((9, rows, LANES), F32),
            pltpu.VMEM((8, rows, LANES), F32),
            pltpu.VMEM((8 * rows, LANES), BF16),
        ],
        compiler_params=limits(24),
        cost_estimate=cost(2 * 8 * 4 * rows * rows * 2 * LANES, 0),
    )(ids, *grads, spec, *tables)


def finish(ids, lows, highs, key, value, factor):
    shape = key.shape
    return pl.pallas_call(
        functools.partial(finish_kernel, factor),
        out_shape=[jax.ShapeDtypeStruct(shape, BF16), jax.ShapeDtypeStruct(shape, BF16), jax.ShapeDtypeStruct(shape, F32)],
        in_specs=[SMEM] + [VMEM] * 10,
        out_specs=[VMEM] * 3,
        compiler_params=limits(24),
        cost_estimate=cost(4 * key.size, 16 * key.size),
    )(ids, *lows, *highs, key, value)


PRECISION = lax.Precision.HIGH


def dft_tables(period):
    indices = jnp.arange(period, dtype=jnp.int32)
    product = indices[:, None] * indices[None, :] % period
    angles = product.astype(jnp.float32) * (2.0 * math.pi / period)
    return (jnp.cos(angles), jnp.sin(angles))


def spectrum(cosine_table, sine_table, framed_blocks):
    real_component = jnp.einsum(
        "br,irh->ibh", cosine_table, framed_blocks, precision=PRECISION
    )
    imaginary_component = -jnp.einsum(
        "br,irh->ibh", sine_table, framed_blocks, precision=PRECISION
    )
    return (real_component, imaginary_component)


def padded_spectrum(cosine_table, sine_table, blocks):
    framed_blocks = jnp.concatenate([blocks, jnp.zeros_like(blocks)], axis=1)
    return spectrum(cosine_table, sine_table, framed_blocks)


def inverse_rows(cosine_table, sine_table, real_component, imaginary_component, period):
    first_operand = jnp.einsum(
        "ir,qrb->qib", cosine_table, real_component, precision=PRECISION
    )
    second_operand = jnp.einsum(
        "ir,qrb->qib", sine_table, imaginary_component, precision=PRECISION
    )
    return (first_operand - second_operand) / period


def general_layer(query_gate, key_proj, value_proj, output_grad, output_weight, filter_taps):
    length = query_gate.shape[0]
    channels = query_gate.shape[1]
    period = 2 * length
    members = lax.axis_size("ctx")
    position = lax.axis_index("ctx")
    cosine_table, sine_table = dft_tables(period)
    mixed_grad = lax.dot_general(
        lax.all_gather(output_grad, "ch", axis=1, tiled=True),
        output_weight,
        (((1,), (1,)), ((), ())),
        preferred_element_type=jnp.float32,
    )
    conv_grad = (query_gate.astype(jnp.float32) * mixed_grad).astype(jnp.bfloat16)
    conv_grad = lax.optimization_barrier(conv_grad)
    product = (key_proj.astype(jnp.float32) * value_proj.astype(jnp.float32)).astype(jnp.bfloat16)
    product = lax.optimization_barrier(product)
    inner = product.astype(jnp.float32)
    inner_re, inner_im = padded_spectrum(cosine_table, sine_table, inner[None])
    inner_re = inner_re[0]
    inner_im = inner_im[0]
    whole_taps = lax.all_gather(filter_taps, "ctx", axis=0, tiled=True).astype(jnp.float32)
    leading = jnp.zeros((length, channels), jnp.float32)
    tap_blocks = jnp.concatenate([leading, whole_taps], axis=0).reshape(
        members + 1, length, channels
    )
    segments = jnp.concatenate([tap_blocks[:-1], tap_blocks[1:]], axis=1)
    segment_real, segment_imaginary = spectrum(cosine_table, sine_table, segments)
    lane_ids = jnp.arange(members, dtype=jnp.int32)
    blocks = (
        lax.all_gather(conv_grad, "ctx", axis=0, tiled=True)
        .astype(jnp.float32)
        .reshape(-1, length, channels)
    )
    anchor = jnp.arange(blocks.shape[0], dtype=jnp.int32)
    grad_re, grad_im = padded_spectrum(cosine_table, sine_table, blocks)
    offset = anchor - position
    select_entries = (offset[:, None] == lane_ids[None, :]).astype(jnp.float32)
    filter_tap_real = jnp.einsum(
        "so,owz->swz", select_entries, segment_real, precision=PRECISION
    )
    filter_tap_imaginary = jnp.einsum(
        "so,owz->swz", select_entries, segment_imaginary, precision=PRECISION
    )
    input_re = jnp.sum(filter_tap_real * grad_re + filter_tap_imaginary * grad_im, axis=0)
    input_im = jnp.sum(filter_tap_real * grad_im - filter_tap_imaginary * grad_re, axis=0)
    cross_re = inner_re * grad_re + inner_im * grad_im
    cross_im = inner_re * grad_im - inner_im * grad_re
    lagged = inverse_rows(cosine_table, sine_table, cross_re, cross_im, period)
    before = ((offset - 1)[:, None] == lane_ids[None, :]).astype(jnp.float32)
    upper = jnp.einsum(
        "pn,plc->nlc", select_entries, lagged[:, :length], precision=PRECISION
    )
    lower = jnp.einsum("pn,plc->nlc", before, lagged[:, length:], precision=PRECISION)
    input_grad = jnp.dot(
        cosine_table[length:], input_re, precision=PRECISION
    ) - jnp.dot(sine_table[length:], input_im, precision=PRECISION)
    input_grad = input_grad / period
    grad_key = (value_proj.astype(jnp.float32) * input_grad).astype(jnp.bfloat16)
    grad_value = (key_proj.astype(jnp.float32) * input_grad).astype(jnp.bfloat16)
    factor = 1.0 / math.sqrt(members * length)
    summed = lax.psum_scatter(
        (upper + lower).reshape(members * length, channels).astype(jnp.bfloat16),
        "ctx",
        scatter_dimension=0,
        tiled=True,
    ).astype(jnp.float32)
    grad_taps = summed * factor
    return (grad_key, grad_value, grad_taps)


HINT = 5e9
def hop(x, axis, distance):
    n = lax.axis_size(axis)
    return lax.ppermute(x, axis, [(j, j ^ distance) for j in range(n)])


def exchanged_layer(query_gate, key_proj, value_proj, output_grad, output_weight, filter_taps):
    length, channels = query_gate.shape
    parts = lax.axis_size("ctx")
    tables = [jnp.asarray(t) for t in spectral_tables(2 * parts * length)]
    ids = jnp.stack([lax.axis_index("ctx"), lax.axis_index("ch")]).astype(jnp.int32)
    half = length // 2
    from_x, from_y, from_core = hop(output_grad, "ch", 2), hop(output_grad, "ch", 4), hop(output_grad, "ch", 1)
    sent = pack(filter_taps, key_proj, value_proj, parts)
    series = lax.all_to_all(sent, "ctx", 0, 0, tiled=True).reshape(parts * length, 2 * LANES)
    low_spec, high_spec = [block_spectrum(series, lane, tables[0], tables[1]) for lane in (0, LANES)]
    far_top, far_low = hop(from_y[:half], "ch", 2), hop(from_x[half:], "ch", 4)
    core_x, core_y = hop(from_x, "ch", 1), hop(from_y, "ch", 1)
    total, turned = project_near(ids, output_weight, [output_grad, from_core, from_x, core_x, from_y, core_y], HINT)
    far_top, far_low, total = lax.optimization_barrier((far_top, far_low, total))
    core_top, core_low = hop(far_top, "ch", 1), hop(far_low, "ch", 1)
    grads = project_far(ids, turned, [far_top, core_top, far_low, core_low], total, query_gate)
    spread = lambda blocks: [blocks[0]] + [hop(blocks[s], "ctx", s) for s in range(1, parts)]
    low_grads, high_grads = spread(grads[:parts]), spread(grads[parts:])
    low = spread(correlate(ids, low_grads, low_spec, tables))
    high = spread(correlate(ids, high_grads, high_spec, tables))
    return tuple(finish(ids, low, high, key_proj, value_proj, 1.0 / math.sqrt(parts * length)))


def per_device(*arrays):
    length, channels = arrays[0].shape
    if lax.axis_size("ctx") == 4 and lax.axis_size("ch") == 8 and channels == 4 * LANES and length % 32 == 0:
        return exchanged_layer(*arrays)
    return general_layer(*arrays)


def solution(mesh):
    return jax.shard_map(
        per_device,
        mesh=mesh,
        in_specs=(
            P("ctx", "ch"),
            P("ctx", "ch"),
            P("ctx", "ch"),
            P("ctx", "ch"),
            P("ch", None),
            P("ctx", "ch"),
        ),
        out_specs=(P("ctx", "ch"), P("ctx", "ch"), P("ctx", "ch")),
        check_vma=False,
    )
```

```python
import functools
import math

import jax
import jax.numpy as jnp
import ml_dtypes
import numpy as np
from jax import lax
from jax.experimental import pallas as pl
from jax.experimental.pallas import tpu as pltpu
from jax.sharding import PartitionSpec as P

BF16, F32 = jnp.bfloat16, jnp.float32
FOLDS = 16
LANES = 128


def spectral_tables(period):
    rows = period // FOLDS
    half = rows // 2
    place = np.arange(rows, dtype=np.int64)

    def angles(r):
        return 2.0 * np.pi * ((np.outer(FOLDS * place + r, place)) % period) / period

    forward_real = np.zeros((2, rows, rows))
    backward_real = np.zeros((2, rows, rows))
    for slot, r in ((0, 0), (1, FOLDS // 2)):
        a = angles(r)
        table = np.concatenate([np.cos(a[:half]), -np.sin(a[:half])], axis=0)
        if r == 0:
            table[half] = np.cos(a[half])
        forward_real[slot] = table
        inverse = table.T.copy()
        if r == 0:
            inverse[:, 0] *= 0.5
            inverse[:, half] *= 0.5
        backward_real[slot] = inverse
    forward, backward = [], []
    for r in range(1, FOLDS // 2):
        a = angles(r)
        forward.append(np.concatenate([np.cos(a), np.sin(a)], axis=0))
        backward.append(np.concatenate([np.cos(a).T, np.sin(a).T], axis=0))
    held = lambda t: np.asarray(t).astype(ml_dtypes.bfloat16)
    return held(forward_real), held(np.stack(forward)), held(backward_real), held(np.stack(backward))


def total(terms):
    terms = [t for t in terms if t is not None]
    while len(terms) > 1:
        terms = [a + b for a, b in zip(terms[::2], terms[1::2])] + ([terms[-1]] if len(terms) % 2 else [])
    return terms[0]


C1, S1, C2 = math.cos(math.pi / 8), math.sin(math.pi / 8), math.sqrt(0.5)


def fold_forward(x):
    u = [x[j] + x[j + 4] for j in range(4)]
    v = [x[j] - x[j + 4] for j in range(4)]
    u02, u13 = u[0] + u[2], u[1] + u[3]
    y = [None] * 9
    y[0] = (u02 + u13, None)
    y[8] = (u02 - u13, None)
    y[4] = (u[0] - u[2], u[3] - u[1])
    a, b = C2 * (v[1] - v[3]), C2 * (v[1] + v[3])
    y[2] = (v[0] + a, -(v[2] + b))
    y[6] = (v[0] - a, v[2] - b)
    for r, partner, sign, turns in ((1, 7, -1.0, ((C1, S1), (C2, C2), (S1, C1))), (3, 5, 1.0, ((S1, C1), (-C2, C2), (-C1, -S1)))):
        re, im = [x[0]], [x[4] if sign > 0 else -x[4]]
        for j, (c, s) in zip((1, 2, 3), turns):
            p, q = x[j], x[j + 4]
            if sign < 0:
                re.append(c * p - s * q)
                im.append(-(s * p + c * q))
            else:
                re.append(c * p + s * q)
                im.append(c * q - s * p)
        er, orr = re[0] + re[2], re[1] + re[3]
        ei, oi = im[0] + im[2], im[1] + im[3]
        y[r] = (er + orr, ei + oi)
        y[partner] = (er - orr, oi - ei)
    return y


def fold_backward(z):
    out = [None] * 8
    for parity in (0, 1):
        sign = 1.0 - 2.0 * parity
        a = {}
        for r in (1, 2, 3):
            zr, zi = z[r]
            pr, pi = z[8 - r]
            a[r] = (zr + pr, zi - pi) if parity == 0 else (zr - pr, zi + pi)
        base = z[0][0] + z[8][0] if parity == 0 else z[0][0] - z[8][0]
        z4r, z4i = z[4]
        a1r, a1i = a[1]
        a2r, a2i = a[2]
        a3r, a3i = a[3]
        if parity == 0:
            p0, p1 = base + z4r, base - z4r
            q0, q1 = p0 + a2r, p0 - a2r
            t0, t1 = p1 - a2i, p1 + a2i
            s = a1r + a3r
            out[0], d = q0 + s, None
            out[4] = q1 - a1i + a3i
            m, n = C2 * (a1r - a3r), C2 * (a1i + a3i)
            out[2] = t0 + m - n
            out[6] = t1 - m - n
        else:
            p0, p1 = base - z4i, base + z4i
            m, n = C2 * a2r, C2 * a2i
            e = {1: p0 + m - n, 3: p1 - m - n, 5: p0 - m + n, 7: p1 + m + n}
            c1r, s1r, c1i, s1i = C1 * a1r, S1 * a1r, C1 * a1i, S1 * a1i
            c3r, s3r, c3i, s3i = C1 * a3r, S1 * a3r, C1 * a3i, S1 * a3i
            out[1] = e[1] + (c1r - s1i) + (s3r - c3i)
            out[3] = e[3] + (s1r - c1i) + (-c3r + s3i)
            out[5] = e[5] + (-s1r - c1i) + (c3r + s3i)
            out[7] = e[7] + (-c1r - s1i) + (-s3r - c3i)
    return out


HALF = LANES // 2


def low_lanes(shape):
    return lax.broadcasted_iota(jnp.int32, shape, 1) < HALF


def swap_halves(a):
    return pltpu.roll(a, HALF, 1)


def join_low(a, b):
    return jnp.where(low_lanes(a.shape), a, swap_halves(b))


def join_high(a, b):
    return jnp.where(low_lanes(a.shape), swap_halves(a), b)


def pack_kernel(taps_hbm, key_hbm, value_hbm, out_hbm, taps_ref, key_ref, value_ref, out_ref, in_sems, out_sems):
    parts = out_ref.shape[0]
    reads = []
    for j in range(parts):
        cols = pl.ds(j * LANES, LANES)
        for i, (src, dst) in enumerate(((key_hbm, key_ref), (value_hbm, value_ref), (taps_hbm, taps_ref))):
            reads.append(pltpu.make_async_copy(src.at[:, cols], dst.at[j], in_sems.at[i, j]))
            reads[-1].start()
    writes = []
    for j in range(parts):
        for read in reads[3 * j : 3 * j + 3]:
            read.wait()
        inner = key_ref[j].astype(F32) * value_ref[j].astype(F32)
        taps = taps_ref[j].astype(F32)
        out_ref[j, :, :LANES] = join_low(taps, inner).astype(BF16)
        out_ref[j, :, LANES:] = join_high(taps, inner).astype(BF16)
        writes.append(pltpu.make_async_copy(out_ref.at[j], out_hbm.at[j], out_sems.at[j]))
        writes[-1].start()
    for write in writes:
        write.wait()


def fold_into(y_ref, x_ref, lane=0):
    rows, step = y_ref.shape[1], 16

    def fold(i, carry):
        at = pl.multiple_of(i * step, step)
        y = fold_forward([x_ref[pl.ds(j * rows + at, step), lane : lane + LANES].astype(F32) for j in range(8)])
        for r in range(8):
            left, right = y[r] if r else (y[0][0], y[8][0])
            y_ref[r, pl.ds(at, step), :LANES] = left.astype(BF16)
            y_ref[r, pl.ds(at, step), LANES:] = right.astype(BF16)
        return carry

    lax.fori_loop(0, rows // step, fold, 0, unroll=rows // step)


def dot(a, b):
    return jnp.dot(a, b, preferred_element_type=F32)


def spectrum_kernel(lane, x_ref, real_ref, table_ref, out_ref, y_ref):
    rows = real_ref.shape[1]
    fold_into(y_ref, x_ref, lane)
    out_ref[0, :rows] = dot(real_ref[0], y_ref[0, :, :LANES]).astype(out_ref.dtype)
    out_ref[0, rows:] = dot(real_ref[1], y_ref[0, :, LANES:]).astype(out_ref.dtype)
    for r in range(1, 8):
        d = dot(table_ref[r - 1], y_ref[r])
        out_ref[r, :rows] = (d[:rows, :LANES] + d[rows:, LANES:]).astype(out_ref.dtype)
        out_ref[r, rows:] = (d[:rows, LANES:] - d[rows:, :LANES]).astype(out_ref.dtype)


def correlate_kernel(ids_ref, g0, g1, g2, g3, spec_ref, fr_ref, f_ref, br_ref, b_ref, o0, o1, o2, o3, x_ref, y_ref, zr_ref, zi_ref, res_ref):
    rows = fr_ref.shape[1]
    half = rows // 2
    length = 2 * rows
    step = 16
    z = ids_ref[0]
    for s, g in enumerate((g0, g1, g2, g3)):
        start = pl.multiple_of((z ^ s) * length, length)
        both = g[...].astype(F32)
        x_ref[pl.ds(start, rows), :] = join_low(both, both).astype(BF16)
        x_ref[pl.ds(start + rows, rows), :] = join_high(both, both).astype(BF16)

    fold_into(y_ref, x_ref)
    beside = lambda a, b: jnp.concatenate([a, b], axis=1).astype(BF16)

    for r in range(1, 8):
        d = dot(f_ref[r - 1], y_ref[r])
        gr = d[:rows, :LANES] + d[rows:, LANES:]
        gi = d[:rows, LANES:] - d[rows:, :LANES]
        ar, ai = spec_ref[r, :rows].astype(F32), spec_ref[r, rows:].astype(F32)
        p = dot(b_ref[r - 1], beside(ar * gr + ai * gi, ar * gi - ai * gr))
        zr_ref[r] = p[:rows, :LANES] - p[rows:, LANES:]
        zi_ref[r] = p[:rows, LANES:] + p[rows:, :LANES]
    first = lax.broadcasted_iota(jnp.int32, (half, LANES), 0) == 0
    for slot, r in ((0, 0), (1, 8)):
        g = dot(fr_ref[slot], y_ref[0, :, slot * LANES : (slot + 1) * LANES])
        a = spec_ref[0, slot * rows : (slot + 1) * rows].astype(F32)
        gr, gi, ar, ai = g[:half], g[half:], a[:half], a[half:]
        pr = ar * gr + ai * gi
        pi = ar * gi - ai * gr
        if slot == 0:
            pr = jnp.where(first, ar * gr, pr)
            pi = jnp.where(first, ai * gi, pi)
        zr_ref[r] = dot(br_ref[slot], jnp.concatenate([pr, pi], axis=0).astype(BF16))
    scale = 1.0 / (FOLDS // 2 * rows)

    def unfold(i, carry):
        at = pl.multiple_of(i * step, step)
        zs = [(zr_ref[r, pl.ds(at, step), :], zi_ref[r, pl.ds(at, step), :] if 0 < r < 8 else None) for r in range(9)]
        for j, out in enumerate(fold_backward(zs)):
            res_ref[pl.ds(j * rows + at, step), :] = (out * scale).astype(BF16)
        return carry

    lax.fori_loop(0, rows // step, unfold, 0, unroll=rows // step)
    for s, o in enumerate((o0, o1, o2, o3)):
        o[...] = res_ref[pl.ds(pl.multiple_of((z ^ s) * length, length), length), :]


def finish_kernel(factor, distances, ids_ref, *refs):
    n = len(distances)
    lows, highs = refs[:n], refs[n : 2 * n]
    key_ref, value_ref = refs[2 * n : 2 * n + 2]
    gk_hbm, gv_hbm, gt_hbm, gk_ref, gv_ref, gt_ref, sems = refs[-7:]
    writes = []
    for i, distance in enumerate(distances):
        low, high = lows[i][...].astype(F32), highs[i][...].astype(F32)
        cols = pl.ds(pl.multiple_of((ids_ref[0] ^ distance) * LANES, LANES), LANES)
        gt_ref[i] = join_high(low, high) * factor
        grad = join_low(low, high)
        gk_ref[i] = (value_ref[:, cols].astype(F32) * grad).astype(BF16)
        gv_ref[i] = (key_ref[:, cols].astype(F32) * grad).astype(BF16)
        for k, (held, out) in enumerate(((gt_ref, gt_hbm), (gk_ref, gk_hbm), (gv_ref, gv_hbm))):
            writes.append(pltpu.make_async_copy(held.at[i], out.at[:, cols], sems.at[k, i]))
            writes[-1].start()
    for write in writes:
        write.wait()


def project_near_kernel(ids_ref, weight_ref, *refs):
    *blocks, sums, turned = refs
    depth = blocks[0].shape[1]

    def weight(distance):
        return weight_ref[:, pl.ds(pl.multiple_of((ids_ref[1] ^ distance) * depth, depth), depth)]

    acc = None
    for distance, block in enumerate(blocks):
        part = lax.dot_general(block[...], weight(distance), (((1,), (1,)), ((), ())), preferred_element_type=F32)
        acc = part if acc is None else acc + part
    sums[...] = acc
    for i in range(2):
        turned[i * depth : (i + 1) * depth] = weight(len(blocks) + i).T


def project_far_kernel(ids_ref, turned_ref, top0, top1, low0, low1, before, gate, o0, o1, o2, o3, sums, block):
    half, depth = top0.shape
    for i, (top, low) in enumerate(((top0, low0), (top1, low1))):
        block[:half, i * depth : (i + 1) * depth] = top[...]
        block[half:, i * depth : (i + 1) * depth] = low[...]
    sums[...] = before[...] + dot(block[...], turned_ref[...])
    gate_half(join_low, ids_ref, sums, gate, (o0, o1, o2, o3))


def gate_half(join, ids_ref, sums, gate, outs):
    half = sums.shape[0] // 2
    for s, o in enumerate(outs):
        cols = pl.ds(pl.multiple_of((ids_ref[0] ^ s) * LANES, LANES), LANES)
        grad = gate[:, cols].astype(F32) * sums[:, cols]
        o[...] = join(grad[:half], grad[half:]).astype(BF16)


def gate_high_kernel(ids_ref, sums, gate, o0, o1, o2, o3):
    gate_half(join_high, ids_ref, sums, gate, (o0, o1, o2, o3))


VMEM = pl.BlockSpec(memory_space=pltpu.VMEM)
SMEM = pl.BlockSpec(memory_space=pltpu.SMEM)
ANY = pl.BlockSpec(memory_space=pl.ANY)


def cost(flops, nbytes):
    return pl.CostEstimate(flops=flops, bytes_accessed=nbytes, transcendentals=0)


def limits(mib):
    return pltpu.CompilerParams(vmem_limit_bytes=mib * 2**20)


def project_near(ids, weight, blocks, hint):
    channels = weight.shape[0]
    rows, depth = blocks[0].shape
    return pl.pallas_call(
        project_near_kernel,
        in_specs=[SMEM] + [VMEM] * (1 + len(blocks)),
        out_specs=[VMEM] * 2,
        out_shape=[jax.ShapeDtypeStruct((rows, channels), F32), jax.ShapeDtypeStruct((2 * depth, channels), BF16)],
        compiler_params=limits(24),
        cost_estimate=cost(int(hint), 0),
    )(ids, weight, *blocks)


def project_far(ids, turned, blocks, before, gate):
    rows, channels = gate.shape
    halves = [jax.ShapeDtypeStruct((rows // 2, LANES), BF16)] * (channels // LANES)
    return pl.pallas_call(
        project_far_kernel,
        in_specs=[SMEM] + [VMEM] * 7,
        out_specs=[VMEM] * (len(halves) + 1),
        out_shape=halves + [jax.ShapeDtypeStruct((rows, channels), F32)],
        scratch_shapes=[pltpu.VMEM((rows, turned.shape[0]), BF16)],
        compiler_params=limits(24),
        cost_estimate=cost(2 * rows * turned.size, 0),
    )(ids, turned, *blocks, before, gate)


def gate_high(ids, sums, gate):
    rows, channels = gate.shape
    halves = [jax.ShapeDtypeStruct((rows // 2, LANES), BF16)] * (channels // LANES)
    return pl.pallas_call(
        gate_high_kernel,
        in_specs=[SMEM] + [VMEM] * 2,
        out_specs=[VMEM] * len(halves),
        out_shape=halves,
        compiler_params=limits(24),
        cost_estimate=cost(sums.size, 0),
    )(ids, sums, gate)


def pack(taps, key, value, parts):
    length = taps.shape[0]
    shape = (parts, length, 2 * LANES)
    return pl.pallas_call(
        pack_kernel,
        out_shape=jax.ShapeDtypeStruct(shape, BF16),
        in_specs=[ANY] * 3,
        out_specs=ANY,
        scratch_shapes=[pltpu.VMEM((parts, length, LANES), BF16)] * 3
        + [pltpu.VMEM(shape, BF16), pltpu.SemaphoreType.DMA((3, parts)), pltpu.SemaphoreType.DMA((parts,))],
        compiler_params=limits(56),
        cost_estimate=cost(0, 10 * taps.size),
    )(taps, key, value)


def block_spectrum(x, lane, real, table):
    rows = real.shape[1]
    return pl.pallas_call(
        functools.partial(spectrum_kernel, lane),
        out_shape=jax.ShapeDtypeStruct((8, 2 * rows, LANES), BF16),
        in_specs=[VMEM] * 3,
        out_specs=VMEM,
        scratch_shapes=[pltpu.VMEM((8, rows, 2 * LANES), BF16)],
        compiler_params=limits(24),
        cost_estimate=cost(2 * 8 * 2 * rows * rows * 2 * LANES, 0),
    )(x, real, table)


def correlate(ids, grads, spec, tables):
    rows = tables[0].shape[1]
    length = 2 * rows
    return pl.pallas_call(
        correlate_kernel,
        out_shape=[jax.ShapeDtypeStruct((length, LANES), BF16)] * 4,
        in_specs=[SMEM] + [VMEM] * 9,
        out_specs=[VMEM] * 4,
        scratch_shapes=[
            pltpu.VMEM((8 * rows, LANES), BF16),
            pltpu.VMEM((8, rows, 2 * LANES), BF16),
            pltpu.VMEM((9, rows, LANES), F32),
            pltpu.VMEM((8, rows, LANES), F32),
            pltpu.VMEM((8 * rows, LANES), BF16),
        ],
        compiler_params=limits(24),
        cost_estimate=cost(2 * 8 * 4 * rows * rows * 2 * LANES, 0),
    )(ids, *grads, spec, *tables)


def finish(ids, lows, highs, distances, key, value, factor, before=()):
    length, n = key.shape[0], len(distances)
    ins = [*lows, *highs, key, value, *before]
    held = lambda dtype: pltpu.VMEM((n, length, LANES), dtype)
    return pl.pallas_call(
        functools.partial(finish_kernel, factor, distances),
        out_shape=[jax.ShapeDtypeStruct(key.shape, BF16), jax.ShapeDtypeStruct(key.shape, BF16), jax.ShapeDtypeStruct(key.shape, F32)],
        in_specs=[SMEM] + [VMEM] * (2 * n + 2) + [ANY] * len(before),
        out_specs=[ANY] * 3,
        scratch_shapes=[held(BF16), held(BF16), held(F32), pltpu.SemaphoreType.DMA((3, n))],
        input_output_aliases={2 * n + 3 + i: i for i in range(len(before))},
        compiler_params=limits(24),
        cost_estimate=cost(0, 16 * n * length * LANES),
    )(ids, *ins)


PRECISION = lax.Precision.HIGH


def dft_tables(period):
    indices = jnp.arange(period, dtype=jnp.int32)
    product = indices[:, None] * indices[None, :] % period
    angles = product.astype(jnp.float32) * (2.0 * math.pi / period)
    return (jnp.cos(angles), jnp.sin(angles))


def spectrum(cosine_table, sine_table, framed_blocks):
    real_component = jnp.einsum(
        "br,irh->ibh", cosine_table, framed_blocks, precision=PRECISION
    )
    imaginary_component = -jnp.einsum(
        "br,irh->ibh", sine_table, framed_blocks, precision=PRECISION
    )
    return (real_component, imaginary_component)


def padded_spectrum(cosine_table, sine_table, blocks):
    framed_blocks = jnp.concatenate([blocks, jnp.zeros_like(blocks)], axis=1)
    return spectrum(cosine_table, sine_table, framed_blocks)


def inverse_rows(cosine_table, sine_table, real_component, imaginary_component, period):
    first_operand = jnp.einsum(
        "ir,qrb->qib", cosine_table, real_component, precision=PRECISION
    )
    second_operand = jnp.einsum(
        "ir,qrb->qib", sine_table, imaginary_component, precision=PRECISION
    )
    return (first_operand - second_operand) / period


def general_layer(query_gate, key_proj, value_proj, output_grad, output_weight, filter_taps):
    length = query_gate.shape[0]
    channels = query_gate.shape[1]
    period = 2 * length
    members = lax.axis_size("ctx")
    position = lax.axis_index("ctx")
    cosine_table, sine_table = dft_tables(period)
    mixed_grad = lax.dot_general(
        lax.all_gather(output_grad, "ch", axis=1, tiled=True),
        output_weight,
        (((1,), (1,)), ((), ())),
        preferred_element_type=jnp.float32,
    )
    conv_grad = (query_gate.astype(jnp.float32) * mixed_grad).astype(jnp.bfloat16)
    conv_grad = lax.optimization_barrier(conv_grad)
    product = (key_proj.astype(jnp.float32) * value_proj.astype(jnp.float32)).astype(jnp.bfloat16)
    product = lax.optimization_barrier(product)
    inner = product.astype(jnp.float32)
    inner_re, inner_im = padded_spectrum(cosine_table, sine_table, inner[None])
    inner_re = inner_re[0]
    inner_im = inner_im[0]
    whole_taps = lax.all_gather(filter_taps, "ctx", axis=0, tiled=True).astype(jnp.float32)
    leading = jnp.zeros((length, channels), jnp.float32)
    tap_blocks = jnp.concatenate([leading, whole_taps], axis=0).reshape(
        members + 1, length, channels
    )
    segments = jnp.concatenate([tap_blocks[:-1], tap_blocks[1:]], axis=1)
    segment_real, segment_imaginary = spectrum(cosine_table, sine_table, segments)
    lane_ids = jnp.arange(members, dtype=jnp.int32)
    blocks = (
        lax.all_gather(conv_grad, "ctx", axis=0, tiled=True)
        .astype(jnp.float32)
        .reshape(-1, length, channels)
    )
    anchor = jnp.arange(blocks.shape[0], dtype=jnp.int32)
    grad_re, grad_im = padded_spectrum(cosine_table, sine_table, blocks)
    offset = anchor - position
    select_entries = (offset[:, None] == lane_ids[None, :]).astype(jnp.float32)
    filter_tap_real = jnp.einsum(
        "so,owz->swz", select_entries, segment_real, precision=PRECISION
    )
    filter_tap_imaginary = jnp.einsum(
        "so,owz->swz", select_entries, segment_imaginary, precision=PRECISION
    )
    input_re = jnp.sum(filter_tap_real * grad_re + filter_tap_imaginary * grad_im, axis=0)
    input_im = jnp.sum(filter_tap_real * grad_im - filter_tap_imaginary * grad_re, axis=0)
    cross_re = inner_re * grad_re + inner_im * grad_im
    cross_im = inner_re * grad_im - inner_im * grad_re
    lagged = inverse_rows(cosine_table, sine_table, cross_re, cross_im, period)
    before = ((offset - 1)[:, None] == lane_ids[None, :]).astype(jnp.float32)
    upper = jnp.einsum(
        "pn,plc->nlc", select_entries, lagged[:, :length], precision=PRECISION
    )
    lower = jnp.einsum("pn,plc->nlc", before, lagged[:, length:], precision=PRECISION)
    input_grad = jnp.dot(
        cosine_table[length:], input_re, precision=PRECISION
    ) - jnp.dot(sine_table[length:], input_im, precision=PRECISION)
    input_grad = input_grad / period
    grad_key = (value_proj.astype(jnp.float32) * input_grad).astype(jnp.bfloat16)
    grad_value = (key_proj.astype(jnp.float32) * input_grad).astype(jnp.bfloat16)
    factor = 1.0 / math.sqrt(members * length)
    summed = lax.psum_scatter(
        (upper + lower).reshape(members * length, channels).astype(jnp.bfloat16),
        "ctx",
        scatter_dimension=0,
        tiled=True,
    ).astype(jnp.float32)
    grad_taps = summed * factor
    return (grad_key, grad_value, grad_taps)


HINT = 5e9
def hop(x, axis, distance):
    n = lax.axis_size(axis)
    return lax.ppermute(x, axis, [(j, j ^ distance) for j in range(n)])


def exchanged_layer(query_gate, key_proj, value_proj, output_grad, output_weight, filter_taps):
    length, channels = query_gate.shape
    parts = lax.axis_size("ctx")
    tables = [jnp.asarray(t) for t in spectral_tables(2 * parts * length)]
    ids = jnp.stack([lax.axis_index("ctx"), lax.axis_index("ch")]).astype(jnp.int32)
    half = length // 2
    from_x, from_y, from_core = hop(output_grad, "ch", 2), hop(output_grad, "ch", 4), hop(output_grad, "ch", 1)
    sent = pack(filter_taps, key_proj, value_proj, parts)
    series = lax.all_to_all(sent, "ctx", 0, 0, tiled=True).reshape(parts * length, 2 * LANES)
    low_spec, high_spec = [block_spectrum(series, lane, tables[0], tables[1]) for lane in (0, LANES)]
    far_top, far_low = hop(from_y[:half], "ch", 2), hop(from_x[half:], "ch", 4)
    core_x, core_y = hop(from_x, "ch", 1), hop(from_y, "ch", 1)
    total, turned = project_near(ids, output_weight, [output_grad, from_core, from_x, core_x, from_y, core_y], HINT)
    far_top, far_low, total = lax.optimization_barrier((far_top, far_low, total))
    core_top, core_low = hop(far_top, "ch", 1), hop(far_low, "ch", 1)
    *low_grads, sums = project_far(ids, turned, [far_top, core_top, far_low, core_low], total, query_gate)
    spread = lambda blocks: [blocks[0]] + [hop(blocks[s], "ctx", s) for s in range(1, parts)]
    low_grads, high = spread(low_grads), list(gate_high(ids, sums, query_gate))
    low_spec, high[2], high[3] = lax.optimization_barrier((low_spec, high[2], high[3]))
    high_grads = spread(high)
    low = spread(correlate(ids, low_grads, low_spec, tables))
    high = spread(correlate(ids, high_grads, high_spec, tables))
    factor = 1.0 / math.sqrt(parts * length)
    low[2], low[3], high[1] = lax.optimization_barrier((low[2], low[3], high[1]))
    near = finish(ids, low[:2], high[:2], (0, 1), key_proj, value_proj, factor)
    return tuple(finish(ids, low[2:], high[2:], (2, 3), key_proj, value_proj, factor, near))


def per_device(*arrays):
    length, channels = arrays[0].shape
    if lax.axis_size("ctx") == 4 and lax.axis_size("ch") == 8 and channels == 4 * LANES and length % 32 == 0:
        return exchanged_layer(*arrays)
    return general_layer(*arrays)


def solution(mesh):
    return jax.shard_map(
        per_device,
        mesh=mesh,
        in_specs=(
            P("ctx", "ch"),
            P("ctx", "ch"),
            P("ctx", "ch"),
            P("ctx", "ch"),
            P("ch", None),
            P("ctx", "ch"),
        ),
        out_specs=(P("ctx", "ch"), P("ctx", "ch"), P("ctx", "ch")),
        check_vma=False,
    )
```

```python
import functools
import math

import jax
import jax.numpy as jnp
import ml_dtypes
import numpy as np
from jax import lax
from jax.experimental import pallas as pl
from jax.experimental.pallas import tpu as pltpu
from jax.sharding import PartitionSpec as P

BF16, F32 = jnp.bfloat16, jnp.float32
FOLDS = 16
LANES = 128


def spectral_tables(period):
    rows = period // FOLDS
    half = rows // 2
    place = np.arange(rows, dtype=np.int64)

    def angles(r):
        return 2.0 * np.pi * ((np.outer(FOLDS * place + r, place)) % period) / period

    forward_real = np.zeros((2, rows, rows))
    backward_real = np.zeros((2, rows, rows))
    for slot, r in ((0, 0), (1, FOLDS // 2)):
        a = angles(r)
        table = np.concatenate([np.cos(a[:half]), -np.sin(a[:half])], axis=0)
        if r == 0:
            table[half] = np.cos(a[half])
        forward_real[slot] = table
        inverse = table.T.copy()
        if r == 0:
            inverse[:, 0] *= 0.5
            inverse[:, half] *= 0.5
        backward_real[slot] = inverse
    forward, backward = [], []
    for r in range(1, FOLDS // 2):
        a = angles(r)
        forward.append(np.concatenate([np.cos(a), np.sin(a)], axis=0))
        backward.append(np.concatenate([np.cos(a).T, np.sin(a).T], axis=0))
    held = lambda t: np.asarray(t).astype(ml_dtypes.bfloat16)
    return held(forward_real), held(np.stack(forward)), held(backward_real), held(np.stack(backward))


def total(terms):
    terms = [t for t in terms if t is not None]
    while len(terms) > 1:
        terms = [a + b for a, b in zip(terms[::2], terms[1::2])] + ([terms[-1]] if len(terms) % 2 else [])
    return terms[0]


C1, S1, C2 = math.cos(math.pi / 8), math.sin(math.pi / 8), math.sqrt(0.5)


def fold_forward(x):
    u = [x[j] + x[j + 4] for j in range(4)]
    v = [x[j] - x[j + 4] for j in range(4)]
    u02, u13 = u[0] + u[2], u[1] + u[3]
    y = [None] * 9
    y[0] = (u02 + u13, None)
    y[8] = (u02 - u13, None)
    y[4] = (u[0] - u[2], u[3] - u[1])
    a, b = C2 * (v[1] - v[3]), C2 * (v[1] + v[3])
    y[2] = (v[0] + a, -(v[2] + b))
    y[6] = (v[0] - a, v[2] - b)
    for r, partner, sign, turns in ((1, 7, -1.0, ((C1, S1), (C2, C2), (S1, C1))), (3, 5, 1.0, ((S1, C1), (-C2, C2), (-C1, -S1)))):
        re, im = [x[0]], [x[4] if sign > 0 else -x[4]]
        for j, (c, s) in zip((1, 2, 3), turns):
            p, q = x[j], x[j + 4]
            if sign < 0:
                re.append(c * p - s * q)
                im.append(-(s * p + c * q))
            else:
                re.append(c * p + s * q)
                im.append(c * q - s * p)
        er, orr = re[0] + re[2], re[1] + re[3]
        ei, oi = im[0] + im[2], im[1] + im[3]
        y[r] = (er + orr, ei + oi)
        y[partner] = (er - orr, oi - ei)
    return y


def fold_backward(z):
    out = [None] * 8
    for parity in (0, 1):
        sign = 1.0 - 2.0 * parity
        a = {}
        for r in (1, 2, 3):
            zr, zi = z[r]
            pr, pi = z[8 - r]
            a[r] = (zr + pr, zi - pi) if parity == 0 else (zr - pr, zi + pi)
        base = z[0][0] + z[8][0] if parity == 0 else z[0][0] - z[8][0]
        z4r, z4i = z[4]
        a1r, a1i = a[1]
        a2r, a2i = a[2]
        a3r, a3i = a[3]
        if parity == 0:
            p0, p1 = base + z4r, base - z4r
            q0, q1 = p0 + a2r, p0 - a2r
            t0, t1 = p1 - a2i, p1 + a2i
            s = a1r + a3r
            out[0], d = q0 + s, None
            out[4] = q1 - a1i + a3i
            m, n = C2 * (a1r - a3r), C2 * (a1i + a3i)
            out[2] = t0 + m - n
            out[6] = t1 - m - n
        else:
            p0, p1 = base - z4i, base + z4i
            m, n = C2 * a2r, C2 * a2i
            e = {1: p0 + m - n, 3: p1 - m - n, 5: p0 - m + n, 7: p1 + m + n}
            c1r, s1r, c1i, s1i = C1 * a1r, S1 * a1r, C1 * a1i, S1 * a1i
            c3r, s3r, c3i, s3i = C1 * a3r, S1 * a3r, C1 * a3i, S1 * a3i
            out[1] = e[1] + (c1r - s1i) + (s3r - c3i)
            out[3] = e[3] + (s1r - c1i) + (-c3r + s3i)
            out[5] = e[5] + (-s1r - c1i) + (c3r + s3i)
            out[7] = e[7] + (-c1r - s1i) + (-s3r - c3i)
    return out


HALF = LANES // 2


def low_lanes(shape):
    return lax.broadcasted_iota(jnp.int32, shape, 1) < HALF


def swap_halves(a):
    return pltpu.roll(a, HALF, 1)


def join_low(a, b):
    return jnp.where(low_lanes(a.shape), a, swap_halves(b))


def join_high(a, b):
    return jnp.where(low_lanes(a.shape), swap_halves(a), b)


def pack_kernel(taps_hbm, key_hbm, value_hbm, out_hbm, taps_ref, key_ref, value_ref, out_ref, in_sems, out_sems):
    parts = out_ref.shape[0]
    reads = []
    for j in range(parts):
        cols = pl.ds(j * LANES, LANES)
        for i, (src, dst) in enumerate(((key_hbm, key_ref), (value_hbm, value_ref), (taps_hbm, taps_ref))):
            reads.append(pltpu.make_async_copy(src.at[:, cols], dst.at[j], in_sems.at[i, j]))
            reads[-1].start()
    writes = []
    for j in range(parts):
        for read in reads[3 * j : 3 * j + 3]:
            read.wait()
        inner = key_ref[j].astype(F32) * value_ref[j].astype(F32)
        taps = taps_ref[j].astype(F32)
        lanes = slice(j // 2 * LANES, (j // 2 + 1) * LANES)
        for i, join in enumerate((join_low, join_high)):
            owner = j % 2 * 2 + i
            out_ref[owner, :, lanes] = join(taps, inner).astype(BF16)
            writes.append(pltpu.make_async_copy(out_ref.at[owner, :, lanes], out_hbm.at[owner, :, lanes], out_sems.at[j, i]))
            writes[-1].start()
    for write in writes:
        write.wait()


def fold_into(y_ref, x_ref, lane=0):
    rows, step = y_ref.shape[1], 16

    def fold(i, carry):
        at = pl.multiple_of(i * step, step)
        y = fold_forward([x_ref[pl.ds(j * rows + at, step), lane : lane + LANES].astype(F32) for j in range(8)])
        for r in range(8):
            left, right = y[r] if r else (y[0][0], y[8][0])
            y_ref[r, pl.ds(at, step), :LANES] = left.astype(BF16)
            y_ref[r, pl.ds(at, step), LANES:] = right.astype(BF16)
        return carry

    lax.fori_loop(0, rows // step, fold, 0, unroll=rows // step)


def dot(a, b):
    return jnp.dot(a, b, preferred_element_type=F32)


def spectrum_kernel(lane, x_ref, real_ref, table_ref, out_ref, y_ref):
    rows = real_ref.shape[1]
    fold_into(y_ref, x_ref, lane)
    out_ref[0, :rows] = dot(real_ref[0], y_ref[0, :, :LANES]).astype(out_ref.dtype)
    out_ref[0, rows:] = dot(real_ref[1], y_ref[0, :, LANES:]).astype(out_ref.dtype)
    for r in range(1, 8):
        d = dot(table_ref[r - 1], y_ref[r])
        out_ref[r, :rows] = (d[:rows, :LANES] + d[rows:, LANES:]).astype(out_ref.dtype)
        out_ref[r, rows:] = (d[:rows, LANES:] - d[rows:, :LANES]).astype(out_ref.dtype)


def correlate_kernel(ids_ref, g0, g1, g2, g3, spec_ref, fr_ref, f_ref, br_ref, b_ref, o0, o1, o2, o3, x_ref, y_ref, zr_ref, zi_ref, res_ref):
    rows = fr_ref.shape[1]
    half = rows // 2
    length = 2 * rows
    step = 16
    z = ids_ref[0]
    for s, g in enumerate((g0, g1, g2, g3)):
        start = pl.multiple_of((z ^ s) * length, length)
        both = g[...].astype(F32)
        x_ref[pl.ds(start, rows), :] = join_low(both, both).astype(BF16)
        x_ref[pl.ds(start + rows, rows), :] = join_high(both, both).astype(BF16)

    fold_into(y_ref, x_ref)
    beside = lambda a, b: jnp.concatenate([a, b], axis=1).astype(BF16)

    for r in range(1, 8):
        d = dot(f_ref[r - 1], y_ref[r])
        gr = d[:rows, :LANES] + d[rows:, LANES:]
        gi = d[:rows, LANES:] - d[rows:, :LANES]
        ar, ai = spec_ref[r, :rows].astype(F32), spec_ref[r, rows:].astype(F32)
        p = dot(b_ref[r - 1], beside(ar * gr + ai * gi, ar * gi - ai * gr))
        zr_ref[r] = p[:rows, :LANES] - p[rows:, LANES:]
        zi_ref[r] = p[:rows, LANES:] + p[rows:, :LANES]
    first = lax.broadcasted_iota(jnp.int32, (half, LANES), 0) == 0
    for slot, r in ((0, 0), (1, 8)):
        g = dot(fr_ref[slot], y_ref[0, :, slot * LANES : (slot + 1) * LANES])
        a = spec_ref[0, slot * rows : (slot + 1) * rows].astype(F32)
        gr, gi, ar, ai = g[:half], g[half:], a[:half], a[half:]
        pr = ar * gr + ai * gi
        pi = ar * gi - ai * gr
        if slot == 0:
            pr = jnp.where(first, ar * gr, pr)
            pi = jnp.where(first, ai * gi, pi)
        zr_ref[r] = dot(br_ref[slot], jnp.concatenate([pr, pi], axis=0).astype(BF16))
    scale = 1.0 / (FOLDS // 2 * rows)

    def unfold(i, carry):
        at = pl.multiple_of(i * step, step)
        zs = [(zr_ref[r, pl.ds(at, step), :], zi_ref[r, pl.ds(at, step), :] if 0 < r < 8 else None) for r in range(9)]
        for j, out in enumerate(fold_backward(zs)):
            res_ref[pl.ds(j * rows + at, step), :] = (out * scale).astype(BF16)
        return carry

    lax.fori_loop(0, rows // step, unfold, 0, unroll=rows // step)
    for s, o in enumerate((o0, o1, o2, o3)):
        o[...] = res_ref[pl.ds(pl.multiple_of((z ^ s) * length, length), length), :]


def finish_kernel(factor, firsts, distances, ids_ref, *refs):
    n = len(distances)
    parts = refs[: 2 * n]
    key_ref, value_ref = refs[2 * n : 2 * n + 2]
    gk_hbm, gv_hbm, gt_hbm, gk_ref, gv_ref, gt_ref, sems = refs[-7:]
    writes = []
    for i, distance in enumerate(distances):
        owner = ids_ref[0] ^ distance
        one, other = parts[2 * i][...].astype(F32), parts[2 * i + 1][...].astype(F32)
        even = owner % 2 == 0
        low, high = jnp.where(even, one, other), jnp.where(even, other, one)
        cols = pl.ds(pl.multiple_of((firsts[i] + owner // 2) * LANES, LANES), LANES)
        gt_ref[i] = join_high(low, high) * factor
        grad = join_low(low, high)
        gk_ref[i] = (value_ref[:, cols].astype(F32) * grad).astype(BF16)
        gv_ref[i] = (key_ref[:, cols].astype(F32) * grad).astype(BF16)
        for k, (held, out) in enumerate(((gt_ref, gt_hbm), (gk_ref, gk_hbm), (gv_ref, gv_hbm))):
            writes.append(pltpu.make_async_copy(held.at[i], out.at[:, cols], sems.at[k, i]))
            writes[-1].start()
    for write in writes:
        write.wait()


def project_near_kernel(ids_ref, weight_ref, *refs):
    *blocks, sums, turned = refs
    depth = blocks[0].shape[1]

    def weight(distance):
        return weight_ref[:, pl.ds(pl.multiple_of((ids_ref[1] ^ distance) * depth, depth), depth)]

    acc = None
    for distance, block in enumerate(blocks):
        part = lax.dot_general(block[...], weight(distance), (((1,), (1,)), ((), ())), preferred_element_type=F32)
        acc = part if acc is None else acc + part
    sums[...] = acc
    for i in range(2):
        turned[i * depth : (i + 1) * depth] = weight(len(blocks) + i).T


def project_far_kernel(ids_ref, turned_ref, top0, top1, low0, low1, before, gate, o0, o1, o2, o3, sums, block):
    half, depth = top0.shape
    for i, (top, low) in enumerate(((top0, low0), (top1, low1))):
        block[:half, i * depth : (i + 1) * depth] = top[...]
        block[half:, i * depth : (i + 1) * depth] = low[...]
    sums[...] = before[...] + dot(block[...], turned_ref[...])
    gate_half(0, ids_ref, sums, gate, (o0, o1, o2, o3))


def gate_half(first, ids_ref, sums, gate, outs):
    half = sums.shape[0] // 2
    for s, o in enumerate(outs):
        owner = ids_ref[0] ^ s
        cols = pl.ds(pl.multiple_of((first + owner // 2) * LANES, LANES), LANES)
        grad = gate[:, cols].astype(F32) * sums[:, cols]
        even = owner % 2 == 0
        o[...] = jnp.where(even, join_low(grad[:half], grad[half:]), join_high(grad[:half], grad[half:])).astype(BF16)


def gate_high_kernel(ids_ref, sums, gate, o0, o1, o2, o3):
    gate_half(2, ids_ref, sums, gate, (o0, o1, o2, o3))


VMEM = pl.BlockSpec(memory_space=pltpu.VMEM)
SMEM = pl.BlockSpec(memory_space=pltpu.SMEM)
ANY = pl.BlockSpec(memory_space=pl.ANY)


def cost(flops, nbytes):
    return pl.CostEstimate(flops=flops, bytes_accessed=nbytes, transcendentals=0)


def limits(mib):
    return pltpu.CompilerParams(vmem_limit_bytes=mib * 2**20)


def project_near(ids, weight, blocks, hint):
    channels = weight.shape[0]
    rows, depth = blocks[0].shape
    return pl.pallas_call(
        project_near_kernel,
        in_specs=[SMEM] + [VMEM] * (1 + len(blocks)),
        out_specs=[VMEM] * 2,
        out_shape=[jax.ShapeDtypeStruct((rows, channels), F32), jax.ShapeDtypeStruct((2 * depth, channels), BF16)],
        compiler_params=limits(24),
        cost_estimate=cost(int(hint), 0),
    )(ids, weight, *blocks)


def project_far(ids, turned, blocks, before, gate):
    rows, channels = gate.shape
    halves = [jax.ShapeDtypeStruct((rows // 2, LANES), BF16)] * (channels // LANES)
    return pl.pallas_call(
        project_far_kernel,
        in_specs=[SMEM] + [VMEM] * 7,
        out_specs=[VMEM] * (len(halves) + 1),
        out_shape=halves + [jax.ShapeDtypeStruct((rows, channels), F32)],
        scratch_shapes=[pltpu.VMEM((rows, turned.shape[0]), BF16)],
        compiler_params=limits(24),
        cost_estimate=cost(2 * rows * turned.size, 0),
    )(ids, turned, *blocks, before, gate)


def gate_high(ids, sums, gate):
    rows, channels = gate.shape
    halves = [jax.ShapeDtypeStruct((rows // 2, LANES), BF16)] * (channels // LANES)
    return pl.pallas_call(
        gate_high_kernel,
        in_specs=[SMEM] + [VMEM] * 2,
        out_specs=[VMEM] * len(halves),
        out_shape=halves,
        compiler_params=limits(24),
        cost_estimate=cost(sums.size, 0),
    )(ids, sums, gate)


def pack(taps, key, value, parts):
    length = taps.shape[0]
    shape = (parts, length, 2 * LANES)
    return pl.pallas_call(
        pack_kernel,
        out_shape=jax.ShapeDtypeStruct(shape, BF16),
        in_specs=[ANY] * 3,
        out_specs=ANY,
        scratch_shapes=[pltpu.VMEM((parts, length, LANES), BF16)] * 3
        + [pltpu.VMEM(shape, BF16), pltpu.SemaphoreType.DMA((3, parts)), pltpu.SemaphoreType.DMA((parts, 2))],
        compiler_params=limits(56),
        cost_estimate=cost(0, 10 * taps.size),
    )(taps, key, value)


def block_spectrum(x, lane, real, table):
    rows = real.shape[1]
    return pl.pallas_call(
        functools.partial(spectrum_kernel, lane),
        out_shape=jax.ShapeDtypeStruct((8, 2 * rows, LANES), BF16),
        in_specs=[VMEM] * 3,
        out_specs=VMEM,
        scratch_shapes=[pltpu.VMEM((8, rows, 2 * LANES), BF16)],
        compiler_params=limits(24),
        cost_estimate=cost(2 * 8 * 2 * rows * rows * 2 * LANES, 0),
    )(x, real, table)


def correlate(ids, grads, spec, tables):
    rows = tables[0].shape[1]
    length = 2 * rows
    return pl.pallas_call(
        correlate_kernel,
        out_shape=[jax.ShapeDtypeStruct((length, LANES), BF16)] * 4,
        in_specs=[SMEM] + [VMEM] * 9,
        out_specs=[VMEM] * 4,
        scratch_shapes=[
            pltpu.VMEM((8 * rows, LANES), BF16),
            pltpu.VMEM((8, rows, 2 * LANES), BF16),
            pltpu.VMEM((9, rows, LANES), F32),
            pltpu.VMEM((8, rows, LANES), F32),
            pltpu.VMEM((8 * rows, LANES), BF16),
        ],
        compiler_params=limits(24),
        cost_estimate=cost(2 * 8 * 4 * rows * rows * 2 * LANES, 0),
    )(ids, *grads, spec, *tables)


def finish(ids, parts, firsts, distances, key, value, factor, before=()):
    length, n = key.shape[0], len(distances)
    ins = [*parts, key, value, *before]
    held = lambda dtype: pltpu.VMEM((n, length, LANES), dtype)
    return pl.pallas_call(
        functools.partial(finish_kernel, factor, firsts, distances),
        out_shape=[jax.ShapeDtypeStruct(key.shape, BF16), jax.ShapeDtypeStruct(key.shape, BF16), jax.ShapeDtypeStruct(key.shape, F32)],
        in_specs=[SMEM] + [VMEM] * (2 * n + 2) + [ANY] * len(before),
        out_specs=[ANY] * 3,
        scratch_shapes=[held(BF16), held(BF16), held(F32), pltpu.SemaphoreType.DMA((3, n))],
        input_output_aliases={2 * n + 3 + i: i for i in range(len(before))},
        compiler_params=limits(24),
        cost_estimate=cost(0, 16 * n * length * LANES),
    )(ids, *ins)


PRECISION = lax.Precision.HIGH


def dft_tables(period):
    indices = jnp.arange(period, dtype=jnp.int32)
    product = indices[:, None] * indices[None, :] % period
    angles = product.astype(jnp.float32) * (2.0 * math.pi / period)
    return (jnp.cos(angles), jnp.sin(angles))


def spectrum(cosine_table, sine_table, framed_blocks):
    real_component = jnp.einsum(
        "br,irh->ibh", cosine_table, framed_blocks, precision=PRECISION
    )
    imaginary_component = -jnp.einsum(
        "br,irh->ibh", sine_table, framed_blocks, precision=PRECISION
    )
    return (real_component, imaginary_component)


def padded_spectrum(cosine_table, sine_table, blocks):
    framed_blocks = jnp.concatenate([blocks, jnp.zeros_like(blocks)], axis=1)
    return spectrum(cosine_table, sine_table, framed_blocks)


def inverse_rows(cosine_table, sine_table, real_component, imaginary_component, period):
    first_operand = jnp.einsum(
        "ir,qrb->qib", cosine_table, real_component, precision=PRECISION
    )
    second_operand = jnp.einsum(
        "ir,qrb->qib", sine_table, imaginary_component, precision=PRECISION
    )
    return (first_operand - second_operand) / period


def general_layer(query_gate, key_proj, value_proj, output_grad, output_weight, filter_taps):
    length = query_gate.shape[0]
    channels = query_gate.shape[1]
    period = 2 * length
    members = lax.axis_size("ctx")
    position = lax.axis_index("ctx")
    cosine_table, sine_table = dft_tables(period)
    mixed_grad = lax.dot_general(
        lax.all_gather(output_grad, "ch", axis=1, tiled=True),
        output_weight,
        (((1,), (1,)), ((), ())),
        preferred_element_type=jnp.float32,
    )
    conv_grad = (query_gate.astype(jnp.float32) * mixed_grad).astype(jnp.bfloat16)
    conv_grad = lax.optimization_barrier(conv_grad)
    product = (key_proj.astype(jnp.float32) * value_proj.astype(jnp.float32)).astype(jnp.bfloat16)
    product = lax.optimization_barrier(product)
    inner = product.astype(jnp.float32)
    inner_re, inner_im = padded_spectrum(cosine_table, sine_table, inner[None])
    inner_re = inner_re[0]
    inner_im = inner_im[0]
    whole_taps = lax.all_gather(filter_taps, "ctx", axis=0, tiled=True).astype(jnp.float32)
    leading = jnp.zeros((length, channels), jnp.float32)
    tap_blocks = jnp.concatenate([leading, whole_taps], axis=0).reshape(
        members + 1, length, channels
    )
    segments = jnp.concatenate([tap_blocks[:-1], tap_blocks[1:]], axis=1)
    segment_real, segment_imaginary = spectrum(cosine_table, sine_table, segments)
    lane_ids = jnp.arange(members, dtype=jnp.int32)
    blocks = (
        lax.all_gather(conv_grad, "ctx", axis=0, tiled=True)
        .astype(jnp.float32)
        .reshape(-1, length, channels)
    )
    anchor = jnp.arange(blocks.shape[0], dtype=jnp.int32)
    grad_re, grad_im = padded_spectrum(cosine_table, sine_table, blocks)
    offset = anchor - position
    select_entries = (offset[:, None] == lane_ids[None, :]).astype(jnp.float32)
    filter_tap_real = jnp.einsum(
        "so,owz->swz", select_entries, segment_real, precision=PRECISION
    )
    filter_tap_imaginary = jnp.einsum(
        "so,owz->swz", select_entries, segment_imaginary, precision=PRECISION
    )
    input_re = jnp.sum(filter_tap_real * grad_re + filter_tap_imaginary * grad_im, axis=0)
    input_im = jnp.sum(filter_tap_real * grad_im - filter_tap_imaginary * grad_re, axis=0)
    cross_re = inner_re * grad_re + inner_im * grad_im
    cross_im = inner_re * grad_im - inner_im * grad_re
    lagged = inverse_rows(cosine_table, sine_table, cross_re, cross_im, period)
    before = ((offset - 1)[:, None] == lane_ids[None, :]).astype(jnp.float32)
    upper = jnp.einsum(
        "pn,plc->nlc", select_entries, lagged[:, :length], precision=PRECISION
    )
    lower = jnp.einsum("pn,plc->nlc", before, lagged[:, length:], precision=PRECISION)
    input_grad = jnp.dot(
        cosine_table[length:], input_re, precision=PRECISION
    ) - jnp.dot(sine_table[length:], input_im, precision=PRECISION)
    input_grad = input_grad / period
    grad_key = (value_proj.astype(jnp.float32) * input_grad).astype(jnp.bfloat16)
    grad_value = (key_proj.astype(jnp.float32) * input_grad).astype(jnp.bfloat16)
    factor = 1.0 / math.sqrt(members * length)
    summed = lax.psum_scatter(
        (upper + lower).reshape(members * length, channels).astype(jnp.bfloat16),
        "ctx",
        scatter_dimension=0,
        tiled=True,
    ).astype(jnp.float32)
    grad_taps = summed * factor
    return (grad_key, grad_value, grad_taps)


HINT = 5e9
def hop(x, axis, distance):
    n = lax.axis_size(axis)
    return lax.ppermute(x, axis, [(j, j ^ distance) for j in range(n)])


def exchanged_layer(query_gate, key_proj, value_proj, output_grad, output_weight, filter_taps):
    length, channels = query_gate.shape
    parts = lax.axis_size("ctx")
    tables = [jnp.asarray(t) for t in spectral_tables(2 * parts * length)]
    ids = jnp.stack([lax.axis_index("ctx"), lax.axis_index("ch")]).astype(jnp.int32)
    half = length // 2
    from_x, from_y, from_core = hop(output_grad, "ch", 2), hop(output_grad, "ch", 4), hop(output_grad, "ch", 1)
    sent = pack(filter_taps, key_proj, value_proj, parts)
    series = lax.all_to_all(sent, "ctx", 0, 0, tiled=True).reshape(parts * length, 2 * LANES)
    low_spec, high_spec = [block_spectrum(series, lane, tables[0], tables[1]) for lane in (0, LANES)]
    far_top, far_low = hop(from_y[:half], "ch", 2), hop(from_x[half:], "ch", 4)
    core_x, core_y = hop(from_x, "ch", 1), hop(from_y, "ch", 1)
    total, turned = project_near(ids, output_weight, [output_grad, from_core, from_x, core_x, from_y, core_y], HINT)
    far_top, far_low, total = lax.optimization_barrier((far_top, far_low, total))
    core_top, core_low = hop(far_top, "ch", 1), hop(far_low, "ch", 1)
    *low_grads, sums = project_far(ids, turned, [far_top, core_top, far_low, core_low], total, query_gate)
    spread = lambda blocks: [blocks[0]] + [hop(blocks[s], "ctx", s) for s in range(1, parts)]
    low_grads, high = spread(low_grads), list(gate_high(ids, sums, query_gate))
    low_spec, high[2], high[3] = lax.optimization_barrier((low_spec, high[2], high[3]))
    high_grads = spread(high)
    low = spread(correlate(ids, low_grads, low_spec, tables))
    high = spread(correlate(ids, high_grads, high_spec, tables))
    factor = 1.0 / math.sqrt(parts * length)
    low[2], low[3], high[1] = lax.optimization_barrier((low[2], low[3], high[1]))
    done = finish(ids, [*low, *high[:2]], (0, 0, 2), (0, 2, 0), key_proj, value_proj, factor)
    return tuple(finish(ids, high[2:], (2,), (2,), key_proj, value_proj, factor, done))


def per_device(*arrays):
    length, channels = arrays[0].shape
    if lax.axis_size("ctx") == 4 and lax.axis_size("ch") == 8 and channels == 4 * LANES and length % 32 == 0:
        return exchanged_layer(*arrays)
    return general_layer(*arrays)


def solution(mesh):
    return jax.shard_map(
        per_device,
        mesh=mesh,
        in_specs=(
            P("ctx", "ch"),
            P("ctx", "ch"),
            P("ctx", "ch"),
            P("ctx", "ch"),
            P("ch", None),
            P("ctx", "ch"),
        ),
        out_specs=(P("ctx", "ch"), P("ctx", "ch"), P("ctx", "ch")),
        check_vma=False,
    )
```
